128 devices in a mesh: seg: 32 (over x, y, core), kv: 4 (over z).
Axes of the slice: x: 4, y: 4, z: 4, core: 2. Of those that a mesh axis runs over, the one named last changes fastest.
Arguments:
- queries: bfloat16 [32768, 3584], P('seg', 'kv'), may hold values from -250 to 250
- keys: bfloat16 [32768, 512], P('seg', 'kv'), may hold values from -8 to 8
- values: bfloat16 [32768, 512], P('seg', 'kv'), may hold values from -6 to 6
- out_grad: bfloat16 [32768, 3584], P('seg', 'kv'), may hold values from -96 to 96
- parents: int32 [256], replicated, may hold values from -1 to 255, as said below
Outputs:
- query_grad: bfloat16 [32768, 3584], P(('seg', 'kv'))
- key_grad: bfloat16 [32768, 512], P('seg', 'kv')
- value_grad: bfloat16 [32768, 512], P('seg', 'kv')
The draws below stay inside these ranges and needn't reach their ends.
Inputs may be any that keep to these rules, and one draw needn't show every extreme that they name: Only the first 2 nodes of each aligned run of 8 nodes have children. Following parents from any node reaches a root within 5 steps, and some node needs exactly 5.
All inputs are finite; a program needn't handle non-finite values.
Results may differ from the reference program's by a relative error of at most 0.039.
Values may be sent and summed in bfloat16 or wider, within the bound.
No kernel may reach another device: no remote copies, remote signals or barrier semaphores. Data moves between devices by JAX's collectives and lax.ppermute only.
A program may use at most 128 MiB of HBM per device.

```python
import jax
import jax.numpy as jnp
from jax import lax

D_HEAD = 128
Q_HEADS = 28
KV_HEADS = 4
NODE_LEN = 128
NODES_DEV = 8
STEMS = 2
DEPTH = 6
NODES = 256
TOKENS = 32768
N_SEG = 32


def shaped_keys(key):
    first_key = jax.random.fold_in(key, 0)
    base_values = jnp.clip(jax.random.normal(first_key, (TOKENS, KV_HEADS * D_HEAD), jnp.float32), -6.0, 6.0)
    chosen = (jnp.arange(TOKENS) % NODE_LEN == 1)[:, None]
    return jnp.where(chosen, base_values, base_values)


def draw_keys(key, part):
    shaped = shaped_keys(key)
    return shaped.astype(jnp.bfloat16)


def draw_queries(key, part):
    own_key = jax.random.fold_in(key, 3)
    result = jnp.clip(jax.random.normal(own_key, (TOKENS, Q_HEADS * D_HEAD), jnp.float32), -6.0, 6.0)
    return result.astype(jnp.bfloat16)


def stem_node(stem_index):
    return stem_index // STEMS * NODES_DEV + stem_index % STEMS


def draw_parents(key, part):
    key = jax.random.fold_in(key, 5)
    split_keys = jax.random.split(key, 5)
    stem_count = STEMS * N_SEG
    group_width = 2 * (DEPTH - 1)
    stem_order = jax.random.permutation(split_keys[0], stem_count).astype(jnp.int32)
    placing = jnp.arange(stem_count, dtype=jnp.int32)
    group_start = placing // group_width * group_width
    depth_level = (placing - group_start) // 2
    coin_flip = jax.random.randint(split_keys[1], (stem_count,), 0, 2, dtype=jnp.int32)
    upper_spot = jnp.clip(group_start + 2 * (depth_level - 1) + coin_flip, 0, stem_count - 1)
    linked = jnp.where(depth_level > 0, stem_node(stem_order[upper_spot]), -1).astype(jnp.int32)
    stem_parent = jnp.zeros((stem_count,), jnp.int32).at[stem_order].set(linked)
    node_ids = jnp.arange(NODES, dtype=jnp.int32)
    device_of = node_ids // NODES_DEV
    slot_of = node_ids % NODES_DEV
    leaf_target = jax.random.randint(split_keys[2], (NODES,), 0, stem_count, dtype=jnp.int32)
    deep_spot = 2 * (DEPTH - 2) + jax.random.randint(split_keys[3], (N_SEG,), 0, 2, dtype=jnp.int32)
    deep_parent = stem_node(stem_order[deep_spot])
    deep_slot = STEMS + jax.random.randint(split_keys[4], (N_SEG,), 0, NODES_DEV - STEMS, dtype=jnp.int32)
    leaf_parent = jnp.where(slot_of == deep_slot[device_of], deep_parent[device_of], stem_node(leaf_target))
    stem_value = stem_parent[jnp.minimum(device_of * STEMS + slot_of, stem_count - 1)]
    return jnp.where(slot_of < STEMS, stem_value, leaf_parent).astype(jnp.int32)


def steps_of(key, dims, shards, low, top_value):
    def one(dim, shards_of):
        heights = jax.random.uniform(jax.random.fold_in(jax.random.fold_in(key, 6), dim), (shards_of,), jnp.float32, low / len(shards), top_value / len(shards))
        return jnp.repeat(jnp.exp(heights), dims[dim] // shards_of).reshape((-1,) + (1,) * (len(dims) - dim - 1))

    loudness = one(*shards[0])
    for cut in shards[1:]:
        loudness = loudness * one(*cut)
    return loudness


def noise(key, dims, spread, reach, cuts=(), kind=jnp.bfloat16):
    values = jax.random.normal(key, dims, jnp.float32) * spread
    if len(cuts) > 0:
        values = steps_of(key, dims, cuts, -0.22, 0.18) * values
    return jnp.clip(values, min=-reach, max=reach).astype(kind)


def setup_inputs(seed: int = 0) -> dict:
    splits = jax.random.split(jax.random.key(seed), 6)
    return {
        "queries": draw_queries(jax.random.fold_in(splits[5], 71), 0),
        "keys": draw_keys(jax.random.fold_in(splits[5], 71), 0),
        "values": noise(splits[2], (TOKENS, KV_HEADS * D_HEAD), 1.0, 6.0, ((0, 32), (1, 4))),
        "out_grad": noise(splits[3], (TOKENS, Q_HEADS * D_HEAD), 16.0, 96.0, ((0, 32), (1, 4))),
        "parents": draw_parents(jax.random.fold_in(splits[5], 71), 0),
    }


def parent_step(current, parents):
    labels = jnp.arange(parents.shape[0], dtype=jnp.int32)
    matched = current[:, None] == labels[None, :]
    found_parent = jnp.sum(jnp.where(matched, parents[None, :], 0), axis=1)
    return jnp.where(current >= 0, found_parent, -1).astype(jnp.int32)


def ancestor_table(node_ids, parents):
    columns = [node_ids]
    current = node_ids
    for depth_level in range(DEPTH - 1):
        current = parent_step(current, parents)
        columns.append(current)
    return jnp.stack(columns, axis=1)


def slot_scores(query_heads, key_block, visible, score_scale):
    scores = jnp.einsum("nqhgd,nshd->nhgqs", query_heads.astype(jnp.float32), key_block.astype(jnp.float32))
    return jnp.where(visible, scores * score_scale, -jnp.inf)


def block_grads(queries, keys, values, out_grad, node_ids, parents, stem_keys, stem_values):
    score_scale = D_HEAD ** -0.5
    row_count = queries.shape[0]
    node_count = row_count // NODE_LEN
    kv_heads = keys.shape[1] // D_HEAD
    group_size = queries.shape[1] // D_HEAD // kv_heads
    head_shape = (node_count, NODE_LEN, kv_heads, group_size, D_HEAD)
    query_heads = queries.reshape(head_shape)
    grad_heads = out_grad.reshape(head_shape)
    own_keys = keys.reshape(node_count, NODE_LEN, kv_heads, D_HEAD)
    own_values = values.reshape(node_count, NODE_LEN, kv_heads, D_HEAD)
    ancestry = ancestor_table(node_ids, parents)
    position = jnp.arange(NODE_LEN, dtype=jnp.int32)
    causal = (position[:, None] >= position[None, :])[None, None, None]
    slot_list = []
    for depth_level in range(DEPTH):
        if depth_level == 0:
            slot_list.append((own_keys, own_values, causal, None, None))
        else:
            ancestor = ancestry[:, depth_level]
            live_node = ancestor >= 0
            stem_index = jnp.where(live_node, (ancestor // NODES_DEV) * STEMS + ancestor % NODES_DEV, 0).astype(jnp.int32)
            slot_list.append((stem_keys[stem_index], stem_values[stem_index], live_node[:, None, None, None, None], stem_index, live_node))
    stat_shape = (node_count, kv_heads, group_size, NODE_LEN)
    running_max = jnp.full(stat_shape, -jnp.inf, jnp.float32)
    running_sum = jnp.zeros(stat_shape, jnp.float32)
    for key_block, value_block, visible, stem_index, live_node in slot_list:
        scores = slot_scores(query_heads, key_block, visible, score_scale)
        new_max = jnp.maximum(running_max, jnp.max(scores, axis=-1))
        running_sum = running_sum * jnp.exp(running_max - new_max) + jnp.sum(jnp.exp(scores - new_max[..., None]), axis=-1)
        running_max = new_max
    lse = (running_max + jnp.log(running_sum))[..., None]
    attn_acc = jnp.zeros(head_shape, jnp.float32)
    for key_block, value_block, visible, stem_index, live_node in slot_list:
        scores = slot_scores(query_heads, key_block, visible, score_scale)
        prob_half = jnp.exp(scores - lse).astype(jnp.bfloat16)
        attn_acc = attn_acc + jnp.einsum("nhgqs,nshd->nqhgd", prob_half.astype(jnp.float32), value_block.astype(jnp.float32))
    attn_out = attn_acc.astype(jnp.bfloat16)
    delta_rows = jnp.sum(grad_heads.astype(jnp.float32) * attn_out.astype(jnp.float32), axis=-1)
    delta_rows = jnp.transpose(delta_rows, (0, 2, 3, 1))[..., None]
    query_acc = jnp.zeros(head_shape, jnp.float32)
    own_acc = jnp.zeros((node_count, NODE_LEN, kv_heads, 2 * D_HEAD), jnp.float32)
    stem_acc = jnp.zeros((stem_keys.shape[0], NODE_LEN, kv_heads, 2 * D_HEAD), jnp.float32)
    for key_block, value_block, visible, stem_index, live_node in slot_list:
        scores = slot_scores(query_heads, key_block, visible, score_scale)
        prob_full = jnp.exp(scores - lse)
        prob_half = prob_full.astype(jnp.bfloat16)
        prob_grads = jnp.einsum("nqhgd,nshd->nhgqs", grad_heads.astype(jnp.float32), value_block.astype(jnp.float32))
        score_grads = (prob_full * (prob_grads - delta_rows)).astype(jnp.bfloat16)
        query_acc = query_acc + jnp.einsum("nhgqs,nshd->nqhgd", score_grads.astype(jnp.float32), key_block.astype(jnp.float32))
        key_part = jnp.einsum("nhgqs,nqhgd->nshd", score_grads.astype(jnp.float32), query_heads.astype(jnp.float32))
        value_part = jnp.einsum("nhgqs,nqhgd->nshd", prob_half.astype(jnp.float32), grad_heads.astype(jnp.float32))
        key_value = jnp.concatenate([key_part, value_part], axis=-1)
        if stem_index is None:
            own_acc = own_acc + key_value
        else:
            stem_acc = stem_acc.at[stem_index].add(jnp.where(live_node[:, None, None, None], key_value, 0.0))
    query_full = (query_acc * score_scale).reshape(row_count, -1)
    return query_full, own_acc, stem_acc


def reference(queries, keys, values, out_grad, parents):
    row_count = NODES_DEV * NODE_LEN
    stem_rows = STEMS * NODE_LEN
    key_groups = keys.reshape(N_SEG, row_count, -1)
    value_groups = values.reshape(N_SEG, row_count, -1)
    stem_keys = key_groups[:, :stem_rows].reshape(N_SEG * STEMS, NODE_LEN, KV_HEADS, D_HEAD)
    stem_values = value_groups[:, :stem_rows].reshape(N_SEG * STEMS, NODE_LEN, KV_HEADS, D_HEAD)

    def one_group(stem_total, scan_inputs):
        group_index, query_rows, key_rows, value_rows, grad_rows = scan_inputs
        node_ids = (group_index * NODES_DEV + jnp.arange(NODES_DEV, dtype=jnp.int32)).astype(jnp.int32)
        query_full, own_acc, stem_acc = block_grads(query_rows, key_rows, value_rows, grad_rows, node_ids, parents, stem_keys, stem_values)
        return stem_total + stem_acc, (query_full.astype(jnp.bfloat16), own_acc)

    stem_start = jnp.zeros((N_SEG * STEMS, NODE_LEN, KV_HEADS, 2 * D_HEAD), jnp.float32)
    scan_inputs = (jnp.arange(N_SEG, dtype=jnp.int32), queries.reshape(N_SEG, row_count, -1), key_groups, value_groups, out_grad.reshape(N_SEG, row_count, -1))
    stem_total, (query_parts, own_parts) = lax.scan(one_group, stem_start, scan_inputs)
    stem_total = stem_total.reshape(N_SEG, STEMS, NODE_LEN, KV_HEADS, 2 * D_HEAD)
    total_grads = jnp.concatenate([own_parts[:, :STEMS] + stem_total, own_parts[:, STEMS:]], axis=1)
    key_grad = (total_grads[..., :D_HEAD] * (D_HEAD ** -0.5)).astype(jnp.bfloat16).reshape(TOKENS, KV_HEADS * D_HEAD)
    value_grad = total_grads[..., D_HEAD:].astype(jnp.bfloat16).reshape(TOKENS, KV_HEADS * D_HEAD)
    query_grad = query_parts.reshape(TOKENS, Q_HEADS * D_HEAD)
    return query_grad, key_grad, value_grad
```

```python
import functools

import jax
import jax.numpy as jnp
from jax import lax
from jax.experimental import pallas as pl
from jax.experimental.pallas import tpu as pltpu
from jax.sharding import PartitionSpec as P

D_HEAD = 128
GROUP = 7
NODE_LEN = 128
NODES_DEV = 8
STEMS = 2
DEPTH = 6
SIDE = 4
N_SEG = 32
N_KV = 4
ROWS = NODES_DEV * NODE_LEN
STEM_ROWS = STEMS * NODE_LEN
HALF_STEMS = SIDE * SIDE * STEMS
BLOCK_ROWS = ROWS // N_KV
WIDTH = GROUP * D_HEAD
SCALE = D_HEAD ** (-0.5)
SHIFTS = (1, 3, 2)


def seg_index(x, y, core):
    return ((x % SIDE) * SIDE + y % SIDE) * 2 + core % 2


def shift_pairs(axis_of_core, shift):
    pairs = []
    for x in range(SIDE):
        for y in range(SIDE):
            for core in range(2):
                dx, dy = (shift, 0) if axis_of_core[core] == "x" else (0, shift)
                pairs.append((seg_index(x, y, core), seg_index(x + dx, y + dy, core)))
    return pairs


def core_pairs():
    return [(i, i ^ 1) for i in range(N_SEG)]


def kv_pairs(shift):
    return [(i, (i + shift) % N_KV) for i in range(N_KV)]


def spread(block, axis_of_core):
    parts = [block] + [
        lax.ppermute(block, "seg", shift_pairs(axis_of_core, shift)) for shift in range(1, SIDE)
    ]
    return jnp.concatenate(parts, axis=0)


def gather_stems(block):
    line = spread(block, "xy")
    mine = spread(line, "yx")
    other = lax.ppermute(mine, "seg", core_pairs())
    return mine, other


def fold(blocks, axis_of_core):
    rows = blocks.shape[0] // SIDE
    total = blocks[:rows].astype(jnp.float32)
    for shift in range(1, SIDE):
        sent = blocks[shift * rows : (shift + 1) * rows]
        arrived = lax.ppermute(sent, "seg", shift_pairs(axis_of_core, shift))
        total = total + arrived.astype(jnp.float32)
    return total


def reduce_stems(mine, other):
    arrived = lax.ppermute(other, "seg", core_pairs())
    both = (mine.astype(jnp.float32) + arrived.astype(jnp.float32)).astype(jnp.bfloat16)
    line = fold(both, "yx").astype(jnp.bfloat16)
    return fold(line, "xy")


def stem_place(node, chip_x, chip_y, sign):
    device = node // NODES_DEV
    x = device // (2 * SIDE)
    y = device // 2 % SIDE
    core = device % 2
    rel_x = (sign * (x - chip_x) + SIDE) % SIDE
    rel_y = (sign * (y - chip_y) + SIDE) % SIDE
    spot = jnp.where(core == 0, rel_y * SIDE + rel_x, rel_x * SIDE + rel_y)
    return core, spot * STEMS + node % NODES_DEV


def grads_kernel(
    parents,
    where,
    q_ref,
    g_ref,
    k_ref,
    v_ref,
    mine_ref,
    other_ref,
    dq0_ref,
    dq1_ref,
    dq2_ref,
    dq3_ref,
    own_ref,
    smine_ref,
    sother_ref,
    acc,
    touched,
):
    step = pl.program_id(0)
    seg = where[0]
    kv = where[1]
    chip_x = seg // (2 * SIDE)
    chip_y = seg // 2 % SIDE
    my_core = seg % 2
    slot = step // 2
    part = jnp.where(slot == 3, 0, jnp.where(slot == 2, 3, 2 - slot))
    block = (kv + part) % N_KV
    node = seg * NODES_DEV + block * 2 + step % 2

    @pl.when(step == 0)
    def _():
        for i in range(2 * HALF_STEMS):
            touched[i] = 0

    chain = []
    current = node
    count = jnp.int32(0)
    for _ in range(DEPTH - 1):
        current = jnp.where(current >= 0, parents[jnp.maximum(current, 0)], -1)
        chain.append(jnp.maximum(current, 0))
        count = count + (current >= 0).astype(jnp.int32)

    def stem_block(ancestor):
        core, spot = stem_place(ancestor, chip_x, chip_y, -1)
        return jnp.where(core == my_core, mine_ref[spot], other_ref[spot])

    def run(live):
        keys = [k_ref[...]]
        vals = [v_ref[...]]
        for j in range(live):
            fetched = stem_block(chain[j])
            keys.append(fetched[:, :D_HEAD])
            vals.append(fetched[:, D_HEAD:])
        keys = jnp.concatenate(keys, axis=0)
        vals = jnp.concatenate(vals, axis=0)
        keys_t = keys.T
        heads = [
            (q_ref[:, h * D_HEAD : (h + 1) * D_HEAD], g_ref[:, h * D_HEAD : (h + 1) * D_HEAD])
            for h in range(GROUP)
        ]
        q_all = jnp.concatenate([h[0] for h in heads], axis=0)
        g_all = jnp.concatenate([h[1] for h in heads], axis=0)
        prob_parts = []
        grad_parts = []
        nt = (((1,), (1,)), ((), ()))
        for start in range(0, GROUP, 2):
            stop = min(start + 2, GROUP)
            cols = slice(start * D_HEAD, stop * D_HEAD)
            width = (stop - start) * D_HEAD
            scores = lax.dot_general(keys, q_all[cols], nt, preferred_element_type=jnp.float32)
            scores = scores * SCALE
            key_pos = lax.broadcasted_iota(jnp.int32, (NODE_LEN, width), 0)
            query_pos = lax.broadcasted_iota(jnp.int32, (NODE_LEN, width), 1) % NODE_LEN
            own_scores = jnp.where(key_pos <= query_pos, scores[:NODE_LEN], -jnp.inf)
            if live:
                scores = jnp.concatenate([own_scores, scores[NODE_LEN:]], axis=0)
            else:
                scores = own_scores
            top = jnp.max(scores, axis=0, keepdims=True)
            weights = jnp.exp(scores - top)
            prob = weights * (1.0 / jnp.sum(weights, axis=0, keepdims=True))
            prob_parts.append(prob.astype(jnp.bfloat16))
            prob_grads = lax.dot_general(vals, g_all[cols], nt, preferred_element_type=jnp.float32)
            delta = jnp.sum(prob * prob_grads, axis=0, keepdims=True)
            score_grads = (prob * (prob_grads - delta)).astype(jnp.bfloat16)
            grad_parts.append(score_grads)
            dq_t = jnp.dot(keys_t, score_grads, preferred_element_type=jnp.float32) * SCALE
            for h in range(start, stop):
                piece = dq_t[:, (h - start) * D_HEAD : (h - start + 1) * D_HEAD]
                piece = piece.T.astype(jnp.bfloat16)
                for want, ref in ((0, dq2_ref), (1, dq1_ref), (2, dq3_ref), (3, dq0_ref)):

                    @pl.when(slot == want)
                    def _(ref=ref, piece=piece, h=h):
                        ref[:, h * D_HEAD : (h + 1) * D_HEAD] = piece

        prob_half = jnp.concatenate(prob_parts, axis=1)
        score_half = jnp.concatenate(grad_parts, axis=1)
        dk = jnp.dot(score_half, q_all, preferred_element_type=jnp.float32)
        dv = jnp.dot(prob_half, g_all, preferred_element_type=jnp.float32)
        own_ref[0] = jnp.concatenate([dk[:NODE_LEN], dv[:NODE_LEN]], axis=1)
        for j in range(live):
            core, spot = stem_place(chain[j], chip_x, chip_y, 1)
            place = jnp.where(core == my_core, 0, HALF_STEMS) + spot
            rows = slice((j + 1) * NODE_LEN, (j + 2) * NODE_LEN)
            term = jnp.concatenate([dk[rows], dv[rows]], axis=1)
            seen = touched[place]

            @pl.when(seen == 0)
            def _(place=place, term=term):
                acc[place] = term

            @pl.when(seen != 0)
            def _(place=place, term=term):
                acc[place] += term

            touched[place] = 1

    for live in range(DEPTH):
        pl.when(count == live)(functools.partial(run, live))

    @pl.when(step == NODES_DEV - 1)
    def _():
        for first, ref in ((0, smine_ref), (HALF_STEMS, sother_ref)):

            def store(i, carry, first=first, ref=ref):
                @pl.when(touched[first + i] != 0)
                def _():
                    ref[i] = acc[first + i].astype(jnp.bfloat16)

                @pl.when(touched[first + i] == 0)
                def _():
                    ref[i] = jnp.zeros((NODE_LEN, 2 * D_HEAD), jnp.bfloat16)

                return carry

            lax.fori_loop(0, HALF_STEMS, store, 0)


def node_of(step, where):
    slot = step // 2
    part = jnp.where(slot == 3, 0, jnp.where(slot == 2, 3, 2 - slot))
    return (where[1] + part) % N_KV * 2 + step % 2


def node_grads(parents, where, queries, out_grad, keys, values, mine, other):
    def by_node(step, parents, where):
        return (node_of(step, where), 0)

    def fixed(step, parents, where):
        return (0, 0, 0)

    def half_of(slot):
        return lambda step, parents, where: (jnp.clip(step - 2 * slot, 0, 1), 0)

    stem_shape = (HALF_STEMS, NODE_LEN, 2 * D_HEAD)
    dq_spec = lambda slot: pl.BlockSpec((NODE_LEN, WIDTH), half_of(slot))
    block = jax.ShapeDtypeStruct((BLOCK_ROWS, WIDTH), jnp.bfloat16)
    return pl.pallas_call(
        grads_kernel,
        grid_spec=pltpu.PrefetchScalarGridSpec(
            num_scalar_prefetch=2,
            grid=(NODES_DEV,),
            in_specs=[
                pl.BlockSpec((NODE_LEN, WIDTH), by_node),
                pl.BlockSpec((NODE_LEN, WIDTH), by_node),
                pl.BlockSpec((NODE_LEN, D_HEAD), by_node),
                pl.BlockSpec((NODE_LEN, D_HEAD), by_node),
                pl.BlockSpec(stem_shape, fixed),
                pl.BlockSpec(stem_shape, fixed),
            ],
            out_specs=[
                dq_spec(3),
                dq_spec(1),
                dq_spec(0),
                dq_spec(2),
                pl.BlockSpec(
                    (1, NODE_LEN, 2 * D_HEAD),
                    lambda step, parents, where: (node_of(step, where), 0, 0),
                ),
                pl.BlockSpec(stem_shape, fixed),
                pl.BlockSpec(stem_shape, fixed),
            ],
            scratch_shapes=[
                pltpu.VMEM((2 * HALF_STEMS, NODE_LEN, 2 * D_HEAD), jnp.float32),
                pltpu.SMEM((2 * HALF_STEMS,), jnp.int32),
            ],
        ),
        out_shape=[
            block,
            block,
            block,
            block,
            jax.ShapeDtypeStruct((NODES_DEV, NODE_LEN, 2 * D_HEAD), jnp.float32),
            jax.ShapeDtypeStruct(stem_shape, jnp.bfloat16),
            jax.ShapeDtypeStruct(stem_shape, jnp.bfloat16),
        ],
        compiler_params=pltpu.CompilerParams(vmem_limit_bytes=48 * 1024 * 1024),
        name="node_grads",
    )(parents, where, queries, out_grad, keys, values, mine, other)


def place_kernel(where, a0, a1, a2, a3, out, sems):
    kv = where[1]
    copies = []
    for shift, ref in enumerate((a0, a1, a2, a3)):
        column = pl.multiple_of((kv - shift + N_KV) % N_KV * WIDTH, D_HEAD)
        copies.append(
            pltpu.make_async_copy(ref, out.at[:, pl.ds(column, WIDTH)], sems.at[shift])
        )
    for copy in copies:
        copy.start()
    for copy in copies:
        copy.wait()


def place_blocks(where, blocks):
    return pl.pallas_call(
        place_kernel,
        in_specs=[pl.BlockSpec(memory_space=pltpu.SMEM)] + [pl.BlockSpec(memory_space=pl.ANY)] * 4,
        out_specs=pl.BlockSpec(memory_space=pl.ANY),
        out_shape=jax.ShapeDtypeStruct((BLOCK_ROWS, N_KV * WIDTH), jnp.bfloat16),
        scratch_shapes=[pltpu.SemaphoreType.DMA((4,))],
        name="place_blocks",
    )(where, *blocks)


def per_device(queries, keys, values, out_grad, parents):
    where = jnp.stack([lax.axis_index("seg"), lax.axis_index("kv")]).astype(jnp.int32)
    stem_block = jnp.concatenate([keys[:STEM_ROWS], values[:STEM_ROWS]], axis=1)
    mine, other = gather_stems(stem_block)
    stem_shape = (HALF_STEMS, NODE_LEN, 2 * D_HEAD)
    dq0, dq1, dq2, dq3, own, smine, sother = node_grads(
        parents,
        where,
        queries,
        out_grad,
        keys,
        values,
        mine.reshape(stem_shape),
        other.reshape(stem_shape),
    )
    arrived = [dq0] + [
        lax.ppermute(block, "kv", kv_pairs(shift))
        for shift, block in ((1, dq1), (2, dq2), (3, dq3))
    ]
    query_grad = place_blocks(where, arrived)
    flat = (HALF_STEMS * NODE_LEN, 2 * D_HEAD)
    stem_sum = reduce_stems(smine.reshape(flat), sother.reshape(flat))
    own = own.reshape(ROWS, 2 * D_HEAD)
    total = jnp.concatenate([own[:STEM_ROWS] + stem_sum, own[STEM_ROWS:]], axis=0)
    key_grad = (total[:, :D_HEAD] * SCALE).astype(jnp.bfloat16)
    value_grad = total[:, D_HEAD:].astype(jnp.bfloat16)
    return query_grad, key_grad, value_grad


def solution(mesh):
    placed = (P("seg", "kv"), P("seg", "kv"), P("seg", "kv"), P("seg", "kv"), P())
    return jax.shard_map(
        per_device,
        mesh=mesh,
        in_specs=placed,
        out_specs=(P(("seg", "kv"), None), P("seg", "kv"), P("seg", "kv")),
        check_vma=False,
    )
```

```python
import functools

import jax
import jax.numpy as jnp
from jax import lax
from jax.experimental import pallas as pl
from jax.experimental.pallas import tpu as pltpu
from jax.sharding import PartitionSpec as P

D_HEAD = 128
GROUP = 7
NODE_LEN = 128
NODES_DEV = 8
STEMS = 2
DEPTH = 6
SIDE = 4
N_SEG = 32
N_KV = 4
ROWS = NODES_DEV * NODE_LEN
STEM_ROWS = STEMS * NODE_LEN
HALF_STEMS = SIDE * SIDE * STEMS
BLOCK_ROWS = ROWS // N_KV
WIDTH = GROUP * D_HEAD
SCALE = D_HEAD ** (-0.5)
EXP2_SCALE = SCALE * 1.4426950408889634
SHIFTS = (1, 3, 2)


def seg_index(x, y, core):
    return ((x % SIDE) * SIDE + y % SIDE) * 2 + core % 2


def shift_pairs(axis_of_core, shift):
    pairs = []
    for x in range(SIDE):
        for y in range(SIDE):
            for core in range(2):
                dx, dy = (shift, 0) if axis_of_core[core] == "x" else (0, shift)
                pairs.append((seg_index(x, y, core), seg_index(x + dx, y + dy, core)))
    return pairs


def core_pairs():
    return [(i, i ^ 1) for i in range(N_SEG)]


def kv_pairs(shift):
    return [(i, (i + shift) % N_KV) for i in range(N_KV)]


def spread(block, axis_of_core):
    parts = [block] + [
        lax.ppermute(block, "seg", shift_pairs(axis_of_core, shift)) for shift in range(1, SIDE)
    ]
    return jnp.concatenate(parts, axis=0)


def gather_stems(block):
    line = spread(block, "xy")
    mine = spread(line, "yx")
    other = lax.ppermute(mine, "seg", core_pairs())
    return mine, other


def fold(blocks, axis_of_core):
    rows = blocks.shape[0] // SIDE
    total = blocks[:rows].astype(jnp.float32)
    for shift in range(1, SIDE):
        sent = blocks[shift * rows : (shift + 1) * rows]
        arrived = lax.ppermute(sent, "seg", shift_pairs(axis_of_core, shift))
        total = total + arrived.astype(jnp.float32)
    return total


def reduce_stems(mine, other):
    arrived = lax.ppermute(other, "seg", core_pairs())
    both = (mine.astype(jnp.float32) + arrived.astype(jnp.float32)).astype(jnp.bfloat16)
    line = fold(both, "yx").astype(jnp.bfloat16)
    return fold(line, "xy")


def stem_place(node, chip_x, chip_y, sign):
    device = node // NODES_DEV
    x = device // (2 * SIDE)
    y = device // 2 % SIDE
    core = device % 2
    rel_x = (sign * (x - chip_x) + SIDE) % SIDE
    rel_y = (sign * (y - chip_y) + SIDE) % SIDE
    spot = jnp.where(core == 0, rel_y * SIDE + rel_x, rel_x * SIDE + rel_y)
    return core, spot * STEMS + node % NODES_DEV


def part_of(slot):
    return jnp.where(slot == 3, 0, jnp.where(slot == 2, 3, 2 - slot))


def grads_kernel(
    parents,
    where,
    q_ref,
    g_ref,
    k_ref,
    v_ref,
    mine_ref,
    other_ref,
    dq0_ref,
    dq1_ref,
    dq2_ref,
    dq3_ref,
    own_ref,
    smine_ref,
    sother_ref,
    acc,
    touched,
    dq_buf,
):
    seg = where[0]
    kv = where[1]
    chip_x = seg // (2 * SIDE)
    chip_y = seg // 2 % SIDE
    my_core = seg % 2

    for i in range(2 * HALF_STEMS):
        touched[i] = 0

    def one_node(step, carry):
        slot = step // 2
        block = (kv + part_of(slot)) % N_KV
        local = block * 2 + step % 2
        start = pl.multiple_of(local * NODE_LEN, NODE_LEN)
        node_rows = pl.ds(start, NODE_LEN)
        chain = []
        current = seg * NODES_DEV + local
        count = jnp.int32(0)
        for _ in range(DEPTH - 1):
            current = jnp.where(current >= 0, parents[jnp.maximum(current, 0)], -1)
            chain.append(jnp.maximum(current, 0))
            count = count + (current >= 0).astype(jnp.int32)

        def stem_block(ancestor):
            core, spot = stem_place(ancestor, chip_x, chip_y, -1)
            return jnp.where(core == my_core, mine_ref[spot], other_ref[spot])

        def run(live):
            keys = [k_ref[node_rows, :]]
            vals = [v_ref[node_rows, :]]
            for j in range(live):
                fetched = stem_block(chain[j])
                keys.append(fetched[:, :D_HEAD])
                vals.append(fetched[:, D_HEAD:])
            keys = jnp.concatenate(keys, axis=0)
            vals = jnp.concatenate(vals, axis=0)
            columns = [slice(h * D_HEAD, (h + 1) * D_HEAD) for h in range(GROUP)]
            q_all = jnp.concatenate([q_ref[node_rows, c] for c in columns], axis=0)
            g_all = jnp.concatenate([g_ref[node_rows, c] for c in columns], axis=0)
            nt = (((1,), (1,)), ((), ()))
            scores = lax.dot_general(keys, q_all, nt, preferred_element_type=jnp.float32)
            key_pos = lax.broadcasted_iota(jnp.int32, (NODE_LEN, WIDTH), 0)
            query_pos = lax.broadcasted_iota(jnp.int32, (NODE_LEN, WIDTH), 1) & (NODE_LEN - 1)
            own_scores = jnp.where(key_pos <= query_pos, scores[:NODE_LEN], -jnp.inf)
            if live:
                scores = jnp.concatenate([own_scores, scores[NODE_LEN:]], axis=0)
            else:
                scores = own_scores
            top = jnp.max(scores, axis=0, keepdims=True)
            weights = jnp.exp2((scores - top) * EXP2_SCALE)
            prob = weights * (1.0 / jnp.sum(weights, axis=0, keepdims=True))
            prob_half = prob.astype(jnp.bfloat16)
            prob_grads = lax.dot_general(vals, g_all, nt, preferred_element_type=jnp.float32)
            delta = jnp.sum(prob * prob_grads, axis=0, keepdims=True)
            score_half = (prob * (prob_grads - delta)).astype(jnp.bfloat16)
            dq_t = jnp.dot(keys.T, score_half, preferred_element_type=jnp.float32) * SCALE
            for c in columns:
                dq_buf[:, c] = dq_t[:, c].T.astype(jnp.bfloat16)
            dk = jnp.dot(score_half, q_all, preferred_element_type=jnp.float32)
            dv = jnp.dot(prob_half, g_all, preferred_element_type=jnp.float32)
            own_ref[local] = jnp.concatenate([dk[:NODE_LEN], dv[:NODE_LEN]], axis=1)
            for j in range(live):
                core, spot = stem_place(chain[j], chip_x, chip_y, 1)
                place = jnp.where(core == my_core, 0, HALF_STEMS) + spot
                rows = slice((j + 1) * NODE_LEN, (j + 2) * NODE_LEN)
                term = jnp.concatenate([dk[rows], dv[rows]], axis=1)
                acc[place] = jnp.where(touched[place] != 0, acc[place], 0.0) + term
                touched[place] = 1

        for live in range(DEPTH):
            pl.when(count == live)(functools.partial(run, live))

        block_rows = pl.ds(pl.multiple_of(step % 2 * NODE_LEN, NODE_LEN), NODE_LEN)
        for want, ref in ((0, dq2_ref), (1, dq1_ref), (2, dq3_ref), (3, dq0_ref)):

            @pl.when(slot == want)
            def _(ref=ref):
                ref[block_rows, :] = dq_buf[...]

        return carry

    lax.fori_loop(0, NODES_DEV, one_node, 0)

    for first, ref in ((0, smine_ref), (HALF_STEMS, sother_ref)):

        def store(i, carry, first=first, ref=ref):
            @pl.when(touched[first + i] != 0)
            def _():
                ref[i] = acc[first + i].astype(jnp.bfloat16)

            @pl.when(touched[first + i] == 0)
            def _():
                ref[i] = jnp.zeros((NODE_LEN, 2 * D_HEAD), jnp.bfloat16)

            return carry

        lax.fori_loop(0, HALF_STEMS, store, 0)


def node_grads(parents, where, queries, out_grad, keys, values, mine, other):
    stem_shape = (HALF_STEMS, NODE_LEN, 2 * D_HEAD)
    block = jax.ShapeDtypeStruct((BLOCK_ROWS, WIDTH), jnp.bfloat16)
    smem = pl.BlockSpec(memory_space=pltpu.SMEM)
    vmem = pl.BlockSpec(memory_space=pltpu.VMEM)
    return pl.pallas_call(
        grads_kernel,
        in_specs=[smem] * 2 + [vmem] * 6,
        out_specs=[vmem] * 7,
        out_shape=[
            block,
            block,
            block,
            block,
            jax.ShapeDtypeStruct((NODES_DEV, NODE_LEN, 2 * D_HEAD), jnp.float32),
            jax.ShapeDtypeStruct(stem_shape, jnp.bfloat16),
            jax.ShapeDtypeStruct(stem_shape, jnp.bfloat16),
        ],
        scratch_shapes=[
            pltpu.VMEM((2 * HALF_STEMS, NODE_LEN, 2 * D_HEAD), jnp.float32),
            pltpu.SMEM((2 * HALF_STEMS,), jnp.int32),
            pltpu.VMEM((NODE_LEN, WIDTH), jnp.bfloat16),
        ],
        compiler_params=pltpu.CompilerParams(vmem_limit_bytes=40 * 1024 * 1024),
        name="node_grads",
    )(parents, where, queries, out_grad, keys, values, mine, other)


def place_kernel(where, a0, a1, a2, a3, out):
    kv = where[1]
    for shift, ref in enumerate((a0, a1, a2, a3)):
        column = pl.multiple_of((kv - shift + N_KV) % N_KV * WIDTH, D_HEAD)
        out[:, pl.ds(column, WIDTH)] = ref[...]


def place_blocks(where, blocks):
    rows = BLOCK_ROWS // 4
    return pl.pallas_call(
        place_kernel,
        grid=(4,),
        in_specs=[pl.BlockSpec(memory_space=pltpu.SMEM)]
        + [pl.BlockSpec((rows, WIDTH), lambda i: (i, 0))] * 4,
        out_specs=pl.BlockSpec((rows, N_KV * WIDTH), lambda i: (i, 0)),
        out_shape=jax.ShapeDtypeStruct((BLOCK_ROWS, N_KV * WIDTH), jnp.bfloat16),
        name="place_blocks",
    )(where, *blocks)


def per_device(queries, keys, values, out_grad, parents):
    where = jnp.stack([lax.axis_index("seg"), lax.axis_index("kv")]).astype(jnp.int32)
    stem_block = jnp.concatenate([keys[:STEM_ROWS], values[:STEM_ROWS]], axis=1)
    mine, other = gather_stems(stem_block)
    stem_shape = (HALF_STEMS, NODE_LEN, 2 * D_HEAD)
    dq0, dq1, dq2, dq3, own, smine, sother = node_grads(
        parents,
        where,
        queries,
        out_grad,
        keys,
        values,
        mine.reshape(stem_shape),
        other.reshape(stem_shape),
    )
    arrived = [dq0] + [
        lax.ppermute(block, "kv", kv_pairs(shift))
        for shift, block in ((1, dq1), (2, dq2), (3, dq3))
    ]
    query_grad = place_blocks(where, arrived)
    flat = (HALF_STEMS * NODE_LEN, 2 * D_HEAD)
    stem_sum = reduce_stems(smine.reshape(flat), sother.reshape(flat))
    own = own.reshape(ROWS, 2 * D_HEAD)
    total = jnp.concatenate([own[:STEM_ROWS] + stem_sum, own[STEM_ROWS:]], axis=0)
    key_grad = (total[:, :D_HEAD] * SCALE).astype(jnp.bfloat16)
    value_grad = total[:, D_HEAD:].astype(jnp.bfloat16)
    return query_grad, key_grad, value_grad


def solution(mesh):
    placed = (P("seg", "kv"), P("seg", "kv"), P("seg", "kv"), P("seg", "kv"), P())
    return jax.shard_map(
        per_device,
        mesh=mesh,
        in_specs=placed,
        out_specs=(P(("seg", "kv"), None), P("seg", "kv"), P("seg", "kv")),
        check_vma=False,
    )
```

```python
import functools

import jax
import jax.numpy as jnp
from jax import lax
from jax.experimental import pallas as pl
from jax.experimental.pallas import tpu as pltpu
from jax.sharding import PartitionSpec as P

D_HEAD = 128
GROUP = 7
NODE_LEN = 128
NODES_DEV = 8
STEMS = 2
DEPTH = 6
SIDE = 4
N_SEG = 32
N_KV = 4
ROWS = NODES_DEV * NODE_LEN
STEM_ROWS = STEMS * NODE_LEN
HALF_STEMS = SIDE * SIDE * STEMS
BLOCK_ROWS = ROWS // N_KV
WIDTH = GROUP * D_HEAD
SCALE = D_HEAD ** (-0.5)
EXP2_SCALE = SCALE * 1.4426950408889634
PROB_VMEM = 28 * 1024 * 1024
SCORE_VMEM = 28 * 1024 * 1024


def seg_index(x, y, core):
    return ((x % SIDE) * SIDE + y % SIDE) * 2 + core % 2


def shift_pairs(axis_of_core, shift):
    pairs = []
    for x in range(SIDE):
        for y in range(SIDE):
            for core in range(2):
                dx, dy = (shift, 0) if axis_of_core[core] == "x" else (0, shift)
                pairs.append((seg_index(x, y, core), seg_index(x + dx, y + dy, core)))
    return pairs


def core_pairs():
    return [(i, i ^ 1) for i in range(N_SEG)]


def kv_pairs(shift):
    return [(i, (i + shift) % N_KV) for i in range(N_KV)]


def spread(block, axis_of_core):
    parts = [block] + [
        lax.ppermute(block, "seg", shift_pairs(axis_of_core, shift)) for shift in range(1, SIDE)
    ]
    return jnp.concatenate(parts, axis=0)


def gather_stems(block):
    line = spread(block, "xy")
    mine = spread(line, "yx")
    other = lax.ppermute(mine, "seg", core_pairs())
    shape = (HALF_STEMS, NODE_LEN, D_HEAD)
    return mine.reshape(shape), other.reshape(shape)


def shifted(blocks, axis_of_core):
    rows = blocks.shape[0] // SIDE
    parts = [blocks[:rows]]
    for shift in range(1, SIDE):
        sent = blocks[shift * rows : (shift + 1) * rows]
        parts.append(lax.ppermute(sent, "seg", shift_pairs(axis_of_core, shift)))
    return parts


def reduce_stems(mine, other):
    flat = (HALF_STEMS * NODE_LEN, D_HEAD)
    mine, other = mine.reshape(flat), other.reshape(flat)
    arrived = lax.ppermute(other, "seg", core_pairs())
    both = (mine.astype(jnp.float32) + arrived.astype(jnp.float32)).astype(jnp.bfloat16)
    parts = shifted(both, "yx")
    line = sum(part.astype(jnp.float32) for part in parts).astype(jnp.bfloat16)
    return shifted(line, "xy")


def stem_place(node, chip_x, chip_y, sign):
    device = node // NODES_DEV
    x = device // (2 * SIDE)
    y = device // 2 % SIDE
    core = device % 2
    rel_x = (sign * (x - chip_x) + SIDE) % SIDE
    rel_y = (sign * (y - chip_y) + SIDE) % SIDE
    spot = jnp.where(core == 0, rel_y * SIDE + rel_x, rel_x * SIDE + rel_y)
    return core, spot * STEMS + node % NODES_DEV


def part_of(slot):
    return jnp.where(slot == 3, 0, jnp.where(slot == 2, 3, 2 - slot))


class Tree:
    def __init__(self, parents, where):
        self.parents = parents
        self.seg = where[0]
        self.kv = where[1]
        self.chip_x = self.seg // (2 * SIDE)
        self.chip_y = self.seg // 2 % SIDE
        self.core = self.seg % 2

    def local(self, step):
        return (self.kv + part_of(step // 2)) % N_KV * 2 + step % 2

    def chain(self, local):
        nodes = []
        current = self.seg * NODES_DEV + local
        count = jnp.int32(0)
        for _ in range(DEPTH - 1):
            current = jnp.where(current >= 0, self.parents[jnp.maximum(current, 0)], -1)
            nodes.append(jnp.maximum(current, 0))
            count = count + (current >= 0).astype(jnp.int32)
        return nodes, count

    def fetch(self, ancestor, mine_ref, other_ref):
        core, spot = stem_place(ancestor, self.chip_x, self.chip_y, -1)
        return jnp.where(core == self.core, mine_ref[spot], other_ref[spot])

    def place(self, ancestor):
        core, spot = stem_place(ancestor, self.chip_x, self.chip_y, 1)
        return jnp.where(core == self.core, 0, HALF_STEMS) + spot


COLUMNS = [slice(h * D_HEAD, (h + 1) * D_HEAD) for h in range(GROUP)]
NT = (((1,), (1,)), ((), ()))


def clear(touched):
    for i in range(2 * HALF_STEMS):
        touched[i] = 0


def add_terms(tree, chain, live, grads, acc, touched):
    for j in range(live):
        place = tree.place(chain[j])
        term = grads[(j + 1) * NODE_LEN : (j + 2) * NODE_LEN]
        acc[place] = jnp.where(touched[place] != 0, acc[place], 0.0) + term
        touched[place] = 1


def store_sums(acc, touched, smine_ref, sother_ref):
    for first, ref in ((0, smine_ref), (HALF_STEMS, sother_ref)):

        def store(i, carry, first=first, ref=ref):
            @pl.when(touched[first + i] != 0)
            def _():
                ref[i] = acc[first + i].astype(jnp.bfloat16)

            @pl.when(touched[first + i] == 0)
            def _():
                ref[i] = jnp.zeros((NODE_LEN, D_HEAD), jnp.bfloat16)

            return carry

        lax.fori_loop(0, HALF_STEMS, store, 0)


def stacked(ref, rows):
    return jnp.concatenate([ref[rows, c] for c in COLUMNS], axis=0)


def prob_kernel(
    parents,
    where,
    q_ref,
    g_ref,
    k_ref,
    mine_ref,
    other_ref,
    prob_ref,
    own_ref,
    smine_ref,
    sother_ref,
    acc,
    touched,
):
    tree = Tree(parents, where)
    clear(touched)

    def one_node(step, carry):
        local = tree.local(step)
        chain, count = tree.chain(local)

        def run(live):
            rows = pl.ds(pl.multiple_of(local * NODE_LEN, NODE_LEN), NODE_LEN)
            keys = [k_ref[rows, :]]
            for j in range(live):
                keys.append(tree.fetch(chain[j], mine_ref, other_ref))
            keys = jnp.concatenate(keys, axis=0)
            q_all = stacked(q_ref, rows)
            scores = lax.dot_general(keys, q_all, NT, preferred_element_type=jnp.float32)
            key_pos = lax.broadcasted_iota(jnp.int32, (NODE_LEN, WIDTH), 0)
            query_pos = lax.broadcasted_iota(jnp.int32, (NODE_LEN, WIDTH), 1) & (NODE_LEN - 1)
            own_scores = jnp.where(key_pos <= query_pos, scores[:NODE_LEN], -jnp.inf)
            if live:
                scores = jnp.concatenate([own_scores, scores[NODE_LEN:]], axis=0)
            else:
                scores = own_scores
            top = jnp.max(scores, axis=0, keepdims=True)
            weights = jnp.exp2((scores - top) * EXP2_SCALE)
            prob = weights * (1.0 / jnp.sum(weights, axis=0, keepdims=True))
            prob = prob.astype(jnp.bfloat16)
            prob_ref[step, : (live + 1) * NODE_LEN, :] = prob
            grads = jnp.dot(prob, stacked(g_ref, rows), preferred_element_type=jnp.float32)
            own_ref[local] = grads[:NODE_LEN]
            add_terms(tree, chain, live, grads, acc, touched)

        for live in range(DEPTH):
            pl.when(count == live)(functools.partial(run, live))
        return carry

    lax.fori_loop(0, NODES_DEV, one_node, 0)
    store_sums(acc, touched, smine_ref, sother_ref)


def score_kernel(
    parents,
    where,
    q_ref,
    g_ref,
    k_ref,
    v_ref,
    mine_k_ref,
    other_k_ref,
    mine_v_ref,
    other_v_ref,
    prob_ref,
    dq0_ref,
    dq1_ref,
    dq2_ref,
    dq3_ref,
    own_ref,
    smine_ref,
    sother_ref,
    acc,
    touched,
    dq_buf,
):
    tree = Tree(parents, where)
    clear(touched)

    def one_node(step, carry):
        local = tree.local(step)
        chain, count = tree.chain(local)

        def run(live):
            rows = pl.ds(pl.multiple_of(local * NODE_LEN, NODE_LEN), NODE_LEN)
            keys = [k_ref[rows, :]]
            vals = [v_ref[rows, :]]
            for j in range(live):
                keys.append(tree.fetch(chain[j], mine_k_ref, other_k_ref))
                vals.append(tree.fetch(chain[j], mine_v_ref, other_v_ref))
            keys = jnp.concatenate(keys, axis=0)
            vals = jnp.concatenate(vals, axis=0)
            g_all = stacked(g_ref, rows)
            prob = prob_ref[step, : (live + 1) * NODE_LEN, :].astype(jnp.float32)
            prob_grads = lax.dot_general(vals, g_all, NT, preferred_element_type=jnp.float32)
            delta = jnp.sum(prob * prob_grads, axis=0, keepdims=True)
            score_grads = (prob * (prob_grads - delta)).astype(jnp.bfloat16)
            dq_t = jnp.dot(keys.T, score_grads, preferred_element_type=jnp.float32) * SCALE
            for c in COLUMNS:
                dq_buf[:, c] = dq_t[:, c].T.astype(jnp.bfloat16)
            grads = jnp.dot(score_grads, stacked(q_ref, rows), preferred_element_type=jnp.float32)
            own_ref[local] = grads[:NODE_LEN]
            add_terms(tree, chain, live, grads, acc, touched)

        for live in range(DEPTH):
            pl.when(count == live)(functools.partial(run, live))

        block_rows = pl.ds(pl.multiple_of(step % 2 * NODE_LEN, NODE_LEN), NODE_LEN)
        for want, ref in ((0, dq2_ref), (1, dq1_ref), (2, dq3_ref), (3, dq0_ref)):

            @pl.when(step // 2 == want)
            def _(ref=ref):
                ref[block_rows, :] = dq_buf[...]

        return carry

    lax.fori_loop(0, NODES_DEV, one_node, 0)
    store_sums(acc, touched, smine_ref, sother_ref)


SMEM_SPEC = pl.BlockSpec(memory_space=pltpu.SMEM)
VMEM_SPEC = pl.BlockSpec(memory_space=pltpu.VMEM)
ANY_SPEC = pl.BlockSpec(memory_space=pl.ANY)
STEM_OUT = jax.ShapeDtypeStruct((HALF_STEMS, NODE_LEN, D_HEAD), jnp.bfloat16)
OWN_OUT = jax.ShapeDtypeStruct((NODES_DEV, NODE_LEN, D_HEAD), jnp.float32)
PROB_OUT = jax.ShapeDtypeStruct((NODES_DEV, DEPTH * NODE_LEN, WIDTH), jnp.bfloat16)
NODE_SCRATCH = [
    pltpu.VMEM((2 * HALF_STEMS, NODE_LEN, D_HEAD), jnp.float32),
    pltpu.SMEM((2 * HALF_STEMS,), jnp.int32),
]


def node_probs(parents, where, queries, out_grad, keys, mine, other):
    return pl.pallas_call(
        prob_kernel,
        in_specs=[SMEM_SPEC] * 2 + [VMEM_SPEC] * 5,
        out_specs=[VMEM_SPEC] * 4,
        out_shape=[PROB_OUT, OWN_OUT, STEM_OUT, STEM_OUT],
        scratch_shapes=NODE_SCRATCH,
        compiler_params=pltpu.CompilerParams(vmem_limit_bytes=PROB_VMEM),
        cost_estimate=pl.CostEstimate(flops=10**10, bytes_accessed=2**24, transcendentals=0),
        name="node_probs",
    )(parents, where, queries, out_grad, keys, mine, other)


def node_scores(parents, where, queries, out_grad, keys, values, mine_k, other_k, mine_v, other_v, prob):
    block = jax.ShapeDtypeStruct((BLOCK_ROWS, WIDTH), jnp.bfloat16)
    return pl.pallas_call(
        score_kernel,
        in_specs=[SMEM_SPEC] * 2 + [VMEM_SPEC] * 9,
        out_specs=[VMEM_SPEC] * 7,
        out_shape=[block] * 4 + [OWN_OUT, STEM_OUT, STEM_OUT],
        scratch_shapes=NODE_SCRATCH
        + [
            pltpu.VMEM((NODE_LEN, WIDTH), jnp.bfloat16),
        ],
        compiler_params=pltpu.CompilerParams(vmem_limit_bytes=SCORE_VMEM),
        cost_estimate=pl.CostEstimate(flops=13 * 10**9, bytes_accessed=2**24, transcendentals=0),
        name="node_scores",
    )(parents, where, queries, out_grad, keys, values, mine_k, other_k, mine_v, other_v, prob)


def node_grads(parents, where, queries, out_grad, keys, values, mine, other):
    mine_k, mine_v = mine[..., :D_HEAD], mine[..., D_HEAD:]
    other_k, other_v = other[..., :D_HEAD], other[..., D_HEAD:]
    prob, own_v, smine_v, sother_v = node_probs(parents, where, queries, out_grad, keys, mine_k, other_k)
    dq0, dq1, dq2, dq3, own_k, smine_k, sother_k = node_scores(
        parents, where, queries, out_grad, keys, values, mine_k, other_k, mine_v, other_v, prob
    )
    cat = lambda a, b: jnp.concatenate([a, b], axis=-1)
    return dq0, dq1, dq2, dq3, cat(own_k, own_v), cat(smine_k, smine_v), cat(sother_k, sother_v)


def place_kernel(where, a0, a1, a2, a3, out, sems):
    kv = where[1]
    copies = []
    for shift, ref in enumerate((a0, a1, a2, a3)):
        column = pl.multiple_of((kv - shift + N_KV) % N_KV * WIDTH, D_HEAD)
        copies.append(pltpu.make_async_copy(ref, out.at[:, pl.ds(column, WIDTH)], sems.at[shift]))
    for copy in copies:
        copy.start()
    for copy in copies:
        copy.wait()


def place_blocks(where, blocks):
    return pl.pallas_call(
        place_kernel,
        in_specs=[SMEM_SPEC] + [VMEM_SPEC] * 4,
        out_specs=ANY_SPEC,
        out_shape=jax.ShapeDtypeStruct((BLOCK_ROWS, N_KV * WIDTH), jnp.bfloat16),
        scratch_shapes=[pltpu.SemaphoreType.DMA((N_KV,))],
        name="place_blocks",
    )(where, *blocks)


def total_kernel(scale, own_ref, a0, a1, a2, a3, out_ref):
    stem = sum(ref[...].astype(jnp.float32) for ref in (a0, a1, a2, a3))
    own = own_ref[...]
    out_ref[:STEM_ROWS] = ((own[:STEM_ROWS] + stem) * scale).astype(jnp.bfloat16)
    out_ref[STEM_ROWS:] = (own[STEM_ROWS:] * scale).astype(jnp.bfloat16)


def total_grads(own, terms, scale, name):
    return pl.pallas_call(
        functools.partial(total_kernel, scale),
        in_specs=[VMEM_SPEC] * 5,
        out_specs=VMEM_SPEC,
        out_shape=jax.ShapeDtypeStruct((ROWS, D_HEAD), jnp.bfloat16),
        name=name,
    )(own.reshape(ROWS, D_HEAD), *terms)


def per_device(queries, keys, values, out_grad, parents):
    where = jnp.stack([lax.axis_index("seg"), lax.axis_index("kv")]).astype(jnp.int32)
    mine_k, other_k = gather_stems(keys[:STEM_ROWS])
    mine_v, other_v = gather_stems(values[:STEM_ROWS])
    prob, own_v, smine_v, sother_v = node_probs(
        parents, where, queries, out_grad, keys, mine_k, other_k
    )
    terms_v = reduce_stems(smine_v, sother_v)
    dq0, dq1, dq2, dq3, own_k, smine_k, sother_k = node_scores(
        parents, where, queries, out_grad, keys, values, mine_k, other_k, mine_v, other_v, prob
    )
    arrived = [dq0] + [
        lax.ppermute(block, "kv", kv_pairs(shift))
        for shift, block in ((1, dq1), (2, dq2), (3, dq3))
    ]
    terms_k = reduce_stems(smine_k, sother_k)
    value_grad = total_grads(own_v, terms_v, 1.0, "value_total")
    key_grad = total_grads(own_k, terms_k, SCALE, "key_total")
    query_grad = place_blocks(where, arrived)
    return query_grad, key_grad, value_grad


def solution(mesh):
    placed = (P("seg", "kv"), P("seg", "kv"), P("seg", "kv"), P("seg", "kv"), P())
    return jax.shard_map(
        per_device,
        mesh=mesh,
        in_specs=placed,
        out_specs=(P(("seg", "kv"), None), P("seg", "kv"), P("seg", "kv")),
        check_vma=False,
    )
```

```python
import functools

import jax
import jax.numpy as jnp
from jax import lax
from jax.experimental import pallas as pl
from jax.experimental.pallas import tpu as pltpu
from jax.sharding import PartitionSpec as P

D_HEAD = 128
GROUP = 7
NODE_LEN = 128
NODES_DEV = 8
STEMS = 2
DEPTH = 6
SIDE = 4
N_SEG = 32
N_KV = 4
ROWS = NODES_DEV * NODE_LEN
STEM_ROWS = STEMS * NODE_LEN
HALF_STEMS = SIDE * SIDE * STEMS
PIECE = SIDE * STEMS
BLOCK_ROWS = ROWS // N_KV
WIDTH = GROUP * D_HEAD
SCALE = D_HEAD ** (-0.5)
EXP2_SCALE = SCALE * 1.4426950408889634
SHIFTS = (1, 3, 2)


def seg_index(x, y, core):
    return ((x % SIDE) * SIDE + y % SIDE) * 2 + core % 2


def shift_pairs(axis_of_core, shift):
    pairs = []
    for x in range(SIDE):
        for y in range(SIDE):
            for core in range(2):
                dx, dy = (shift, 0) if axis_of_core[core] == "x" else (0, shift)
                pairs.append((seg_index(x, y, core), seg_index(x + dx, y + dy, core)))
    return pairs


def core_pairs():
    return [(i, i ^ 1) for i in range(N_SEG)]


def kv_pairs(shift):
    return [(i, (i + shift) % N_KV) for i in range(N_KV)]


def spread(block, axis_of_core):
    parts = [block] + [
        lax.ppermute(block, "seg", shift_pairs(axis_of_core, shift)) for shift in range(1, SIDE)
    ]
    return jnp.concatenate(parts, axis=0)


def gather_stems(block):
    line = spread(block, "xy")
    parts = [line] + [
        lax.ppermute(line, "seg", shift_pairs("yx", shift)) for shift in range(1, SIDE)
    ]
    swapped = [lax.ppermute(part, "seg", core_pairs()) for part in parts]
    shape = (PIECE, NODE_LEN, 2 * D_HEAD)
    return [part.reshape(shape) for part in parts + swapped]


def reduce_stems(sums, others):
    flat = (PIECE * NODE_LEN, 2 * D_HEAD)
    sums = [term.reshape(flat) for term in sums]
    parts = []
    for shift in (2, 1, 3, 0):
        arrived = lax.ppermute(sums[SIDE + shift], "seg", core_pairs())
        both = (sums[shift].astype(jnp.float32) + arrived.astype(jnp.float32)).astype(jnp.bfloat16)
        if shift:
            both = lax.ppermute(both, "seg", shift_pairs("yx", shift))
        parts.append(both)
    parts, others = lax.optimization_barrier((parts, others))
    rows = STEM_ROWS
    terms = []
    for shift in range(SIDE):
        cut = slice(shift * rows, (shift + 1) * rows)
        total = sum(part[cut].astype(jnp.float32) for part in parts).astype(jnp.bfloat16)
        if shift:
            total = lax.ppermute(total, "seg", shift_pairs("xy", shift))
        terms.append(total)
    return terms, others


def stem_place(node, chip_x, chip_y, sign):
    device = node // NODES_DEV
    x = device // (2 * SIDE)
    y = device // 2 % SIDE
    core = device % 2
    rel_x = (sign * (x - chip_x) + SIDE) % SIDE
    rel_y = (sign * (y - chip_y) + SIDE) % SIDE
    spot = jnp.where(core == 0, rel_y * SIDE + rel_x, rel_x * SIDE + rel_y)
    return core, spot * STEMS + node % NODES_DEV


def part_of(slot):
    return jnp.where(slot == 3, 0, jnp.where(slot == 2, 3, 2 - slot))


def grads_kernel(
    parents,
    where,
    q_hbm,
    g_hbm,
    k_hbm,
    v_hbm,
    m0_ref,
    m1_ref,
    m2_ref,
    m3_ref,
    o0_ref,
    o1_ref,
    o2_ref,
    o3_ref,
    dq0_ref,
    dq1_ref,
    dq2_ref,
    dq3_ref,
    own_ref,
    sm0_ref,
    sm1_ref,
    sm2_ref,
    sm3_ref,
    so0_ref,
    so1_ref,
    so2_ref,
    so3_ref,
    acc,
    dq_buf,
    stems,
    q_buf,
    g_buf,
    kv_buf,
    sems,
    kv_sems,
):
    seg = where[0]
    kv = where[1]
    chip_x = seg // (2 * SIDE)
    chip_y = seg // 2 % SIDE
    my_core = seg % 2

    def local_of(step):
        return (kv + part_of(step // 2)) % N_KV * 2 + step % 2

    def local_of(step):
        return (kv + part_of(step // 2)) % N_KV * 2 + step % 2

    def node_copies(step):
        rows = pl.ds(pl.multiple_of(local_of(step) * NODE_LEN, NODE_LEN), NODE_LEN)
        return [
            pltpu.make_async_copy(source.at[rows, :], target.at[step], sems.at[i, step])
            for i, (source, target) in enumerate(((q_hbm, q_buf), (g_hbm, g_buf)))
        ]

    kv_copies = [
        pltpu.make_async_copy(source, kv_buf.at[i], kv_sems.at[i])
        for i, source in enumerate((k_hbm, v_hbm))
    ]
    for copy in node_copies(0) + kv_copies:
        copy.start()
    for step in range(1, NODES_DEV):
        for copy in node_copies(step):
            copy.start()

    pieces = (m0_ref, m1_ref, m2_ref, m3_ref, o0_ref, o1_ref, o2_ref, o3_ref)
    for i, piece in enumerate(pieces):
        stems[i * PIECE : (i + 1) * PIECE] = piece[...]

    acc[...] = jnp.zeros(acc.shape, acc.dtype)
    for copy in kv_copies:
        copy.wait()

    def one_node(step, carry):
        slot = step // 2
        local = local_of(step)
        node_rows = pl.ds(pl.multiple_of(local * NODE_LEN, NODE_LEN), NODE_LEN)
        chain = []
        current = seg * NODES_DEV + local
        count = jnp.int32(0)
        for _ in range(DEPTH - 1):
            current = jnp.where(current >= 0, parents[jnp.maximum(current, 0)], -1)
            chain.append(jnp.maximum(current, 0))
            count = count + (current >= 0).astype(jnp.int32)

        for copy in node_copies(step):
            copy.wait()

        def stem_block(ancestor):
            core, spot = stem_place(ancestor, chip_x, chip_y, -1)
            return stems[jnp.where(core == my_core, 0, HALF_STEMS) + spot]

        def run(live):
            keys = [kv_buf[0, node_rows, :]]
            vals = [kv_buf[1, node_rows, :]]
            for j in range(live):
                fetched = stem_block(chain[j])
                keys.append(fetched[:, :D_HEAD])
                vals.append(fetched[:, D_HEAD:])
            keys = jnp.concatenate(keys, axis=0)
            vals = jnp.concatenate(vals, axis=0)
            columns = [slice(h * D_HEAD, (h + 1) * D_HEAD) for h in range(GROUP)]
            q_all = jnp.concatenate([q_buf[step, :, c] for c in columns], axis=0)
            g_all = jnp.concatenate([g_buf[step, :, c] for c in columns], axis=0)
            nt = (((1,), (1,)), ((), ()))
            scores = lax.dot_general(keys, q_all, nt, preferred_element_type=jnp.float32)
            key_pos = lax.broadcasted_iota(jnp.int32, (NODE_LEN, WIDTH), 0)
            query_pos = lax.broadcasted_iota(jnp.int32, (NODE_LEN, WIDTH), 1) & (NODE_LEN - 1)
            own_scores = jnp.where(key_pos <= query_pos, scores[:NODE_LEN], -jnp.inf)
            if live:
                scores = jnp.concatenate([own_scores, scores[NODE_LEN:]], axis=0)
            else:
                scores = own_scores
            top = jnp.max(scores, axis=0, keepdims=True)
            weights = jnp.exp2((scores - top) * EXP2_SCALE)
            prob = weights * (1.0 / jnp.sum(weights, axis=0, keepdims=True))
            prob_half = prob.astype(jnp.bfloat16)
            prob_grads = lax.dot_general(vals, g_all, nt, preferred_element_type=jnp.float32)
            delta = jnp.sum(prob * prob_grads, axis=0, keepdims=True)
            score_half = (prob * (prob_grads - delta)).astype(jnp.bfloat16)
            dq_t = jnp.dot(keys.T, score_half, preferred_element_type=jnp.float32) * SCALE
            for c in columns:
                dq_buf[:, c] = dq_t[:, c].T.astype(jnp.bfloat16)
            dk = jnp.dot(score_half, q_all, preferred_element_type=jnp.float32)
            dv = jnp.dot(prob_half, g_all, preferred_element_type=jnp.float32)
            own_ref[local] = jnp.concatenate([dk[:NODE_LEN], dv[:NODE_LEN]], axis=1)
            for j in range(live):
                core, spot = stem_place(chain[j], chip_x, chip_y, 1)
                place = jnp.where(core == my_core, 0, HALF_STEMS) + spot
                rows = slice((j + 1) * NODE_LEN, (j + 2) * NODE_LEN)
                term = jnp.concatenate([dk[rows], dv[rows]], axis=1)
                acc[place] = (acc[place].astype(jnp.float32) + term).astype(jnp.bfloat16)

        for live in range(DEPTH):
            pl.when(count == live)(functools.partial(run, live))

        block_rows = pl.ds(pl.multiple_of(step % 2 * NODE_LEN, NODE_LEN), NODE_LEN)
        for want, ref in ((0, dq2_ref), (1, dq1_ref), (2, dq3_ref), (3, dq0_ref)):

            @pl.when(slot == want)
            def _(ref=ref):
                ref[block_rows, :] = dq_buf[...]

        return carry

    lax.fori_loop(0, NODES_DEV, one_node, 0)

    sums = (sm0_ref, sm1_ref, sm2_ref, sm3_ref, so0_ref, so1_ref, so2_ref, so3_ref)
    for i, ref in enumerate(sums):
        ref[...] = acc[i * PIECE : (i + 1) * PIECE]


def node_grads(parents, where, queries, out_grad, keys, values, pieces):
    stem_shape = (PIECE, NODE_LEN, 2 * D_HEAD)
    block = jax.ShapeDtypeStruct((BLOCK_ROWS, WIDTH), jnp.bfloat16)
    stay = [
        pltpu.with_memory_space_constraint(array, pltpu.HBM)
        for array in (queries, out_grad, keys, values)
    ]
    smem = pl.BlockSpec(memory_space=pltpu.SMEM)
    vmem = pl.BlockSpec(memory_space=pltpu.VMEM)
    return pl.pallas_call(
        grads_kernel,
        in_specs=[smem] * 2 + [pl.BlockSpec(memory_space=pltpu.HBM)] * 4 + [vmem] * (2 * SIDE),
        out_specs=[vmem] * (5 + 2 * SIDE),
        out_shape=[
            block,
            block,
            block,
            block,
            jax.ShapeDtypeStruct((NODES_DEV, NODE_LEN, 2 * D_HEAD), jnp.float32),
        ]
        + [jax.ShapeDtypeStruct(stem_shape, jnp.bfloat16)] * (2 * SIDE),
        scratch_shapes=[
            pltpu.VMEM((2 * HALF_STEMS, NODE_LEN, 2 * D_HEAD), jnp.bfloat16),
            pltpu.VMEM((NODE_LEN, WIDTH), jnp.bfloat16),
            pltpu.VMEM((2 * HALF_STEMS, NODE_LEN, 2 * D_HEAD), jnp.bfloat16),
            pltpu.VMEM((NODES_DEV, NODE_LEN, WIDTH), jnp.bfloat16),
            pltpu.VMEM((NODES_DEV, NODE_LEN, WIDTH), jnp.bfloat16),
            pltpu.VMEM((2, ROWS, D_HEAD), jnp.bfloat16),
            pltpu.SemaphoreType.DMA((2, NODES_DEV)),
            pltpu.SemaphoreType.DMA((2,)),
        ],
        compiler_params=pltpu.CompilerParams(vmem_limit_bytes=40 * 1024 * 1024),
        name="node_grads",
    )(parents, where, *stay, *pieces)


def place_kernel(where, a0, a1, a2, a3, own_ref, dq_ref, dk_ref, dv_ref, dk_buf, dv_buf, sems):
    kv = where[1]
    copies = []
    for shift, ref in enumerate((a0, a1, a2, a3)):
        column = pl.multiple_of((kv - shift + N_KV) % N_KV * WIDTH, D_HEAD)
        copies.append(pltpu.make_async_copy(ref, dq_ref.at[:, pl.ds(column, WIDTH)], sems.at[shift]))
    for copy in copies:
        copy.start()
    own = own_ref[STEM_ROWS:]
    dk_buf[...] = (own[:, :D_HEAD] * SCALE).astype(jnp.bfloat16)
    dv_buf[...] = own[:, D_HEAD:].astype(jnp.bfloat16)
    for i, (buf, ref) in enumerate(((dk_buf, dk_ref), (dv_buf, dv_ref))):
        copies.append(pltpu.make_async_copy(buf, ref.at[STEM_ROWS:], sems.at[N_KV + i]))
        copies[-1].start()
    for copy in copies:
        copy.wait()


def place_blocks(where, blocks, own):
    vmem = pl.BlockSpec(memory_space=pltpu.VMEM)
    hbm = pl.BlockSpec(memory_space=pltpu.HBM)
    shape = jax.ShapeDtypeStruct((ROWS, D_HEAD), jnp.bfloat16)
    buf = pltpu.VMEM((ROWS - STEM_ROWS, D_HEAD), jnp.bfloat16)
    return pl.pallas_call(
        place_kernel,
        in_specs=[pl.BlockSpec(memory_space=pltpu.SMEM)] + [vmem] * 5,
        out_specs=[hbm] * 3,
        out_shape=[jax.ShapeDtypeStruct((BLOCK_ROWS, N_KV * WIDTH), jnp.bfloat16), shape, shape],
        scratch_shapes=[buf, buf, pltpu.SemaphoreType.DMA((N_KV + 2,))],
        name="place_blocks",
    )(where, *blocks, own)


def total_kernel(own_ref, t0, t1, t2, t3, dk_in, dv_in, dk_ref, dv_ref, dk_buf, dv_buf, sems):
    del dk_in, dv_in
    total = own_ref[:STEM_ROWS] + sum(ref[...].astype(jnp.float32) for ref in (t0, t1, t2, t3))
    dk_buf[...] = (total[:, :D_HEAD] * SCALE).astype(jnp.bfloat16)
    dv_buf[...] = total[:, D_HEAD:].astype(jnp.bfloat16)
    copies = [
        pltpu.make_async_copy(buf, ref.at[:STEM_ROWS], sems.at[i])
        for i, (buf, ref) in enumerate(((dk_buf, dk_ref), (dv_buf, dv_ref)))
    ]
    for copy in copies:
        copy.start()
    for copy in copies:
        copy.wait()


def total_grads(own, terms, dk, dv):
    vmem = pl.BlockSpec(memory_space=pltpu.VMEM)
    hbm = pl.BlockSpec(memory_space=pltpu.HBM)
    shape = jax.ShapeDtypeStruct((ROWS, D_HEAD), jnp.bfloat16)
    buf = pltpu.VMEM((STEM_ROWS, D_HEAD), jnp.bfloat16)
    return pl.pallas_call(
        total_kernel,
        in_specs=[vmem] * 5 + [hbm] * 2,
        out_specs=[hbm] * 2,
        out_shape=[shape] * 2,
        scratch_shapes=[buf, buf, pltpu.SemaphoreType.DMA((2,))],
        input_output_aliases={5: 0, 6: 1},
        name="total_grads",
    )(own, *terms, dk, dv)


def per_device(queries, keys, values, out_grad, parents):
    where = jnp.stack([lax.axis_index("seg"), lax.axis_index("kv")]).astype(jnp.int32)
    stem_block = jnp.concatenate([keys[:STEM_ROWS], values[:STEM_ROWS]], axis=1)
    pieces = gather_stems(stem_block)
    dq0, dq1, dq2, dq3, own, *sums = node_grads(
        parents, where, queries, out_grad, keys, values, pieces
    )
    arrived = [dq0] + [
        lax.ppermute(block, "kv", kv_pairs(shift))
        for shift, block in ((1, dq1), (2, dq2), (3, dq3))
    ]
    terms, first = reduce_stems(sums, [arrived[2]])
    arrived[2] = first[0]
    own = own.reshape(ROWS, 2 * D_HEAD)
    query_grad, key_grad, value_grad = place_blocks(where, arrived, own)
    key_grad, value_grad = total_grads(own, terms, key_grad, value_grad)
    return query_grad, key_grad, value_grad


def solution(mesh):
    placed = (P("seg", "kv"), P("seg", "kv"), P("seg", "kv"), P("seg", "kv"), P())
    return jax.shard_map(
        per_device,
        mesh=mesh,
        in_specs=placed,
        out_specs=(P(("seg", "kv"), None), P("seg", "kv"), P("seg", "kv")),
        check_vma=False,
    )
```

```python
import functools

import jax
import jax.numpy as jnp
from jax import lax
from jax.experimental import pallas as pl
from jax.experimental.pallas import tpu as pltpu
from jax.sharding import PartitionSpec as P

D_HEAD = 128
GROUP = 7
NODE_LEN = 128
NODES_DEV = 8
STEMS = 2
DEPTH = 6
SIDE = 4
N_SEG = 32
N_KV = 4
ROWS = NODES_DEV * NODE_LEN
STEM_ROWS = STEMS * NODE_LEN
NODES = 256
HALF_STEMS = SIDE * SIDE * STEMS
PIECE = SIDE * STEMS
BLOCK_ROWS = ROWS // N_KV
WIDTH = GROUP * D_HEAD
SCALE = D_HEAD ** (-0.5)
EXP2_SCALE = SCALE * 1.4426950408889634
SHIFTS = (1, 3, 2)


def seg_index(x, y, core):
    return ((x % SIDE) * SIDE + y % SIDE) * 2 + core % 2


def shift_pairs(axis_of_core, shift):
    pairs = []
    for x in range(SIDE):
        for y in range(SIDE):
            for core in range(2):
                dx, dy = (shift, 0) if axis_of_core[core] == "x" else (0, shift)
                pairs.append((seg_index(x, y, core), seg_index(x + dx, y + dy, core)))
    return pairs


def core_pairs():
    return [(i, i ^ 1) for i in range(N_SEG)]


def kv_pairs(shift):
    return [(i, (i + shift) % N_KV) for i in range(N_KV)]


def spread(block, axis_of_core):
    parts = [block] + [
        lax.ppermute(block, "seg", shift_pairs(axis_of_core, shift)) for shift in range(1, SIDE)
    ]
    return jnp.concatenate(parts, axis=0)


def gather_stems(block):
    line = spread(block, "xy")
    parts = [line] + [
        lax.ppermute(line, "seg", shift_pairs("yx", shift)) for shift in range(1, SIDE)
    ]
    swapped = [lax.ppermute(part, "seg", core_pairs()) for part in parts]
    shape = (PIECE, NODE_LEN, 2 * D_HEAD)
    return [part.reshape(shape) for part in parts + swapped]


def reduce_stems(sums, others):
    flat = (PIECE * NODE_LEN, 2 * D_HEAD)
    sums = [term.reshape(flat) for term in sums]
    parts = []
    for shift in (2, 1, 3, 0):
        arrived = lax.ppermute(sums[SIDE + shift], "seg", core_pairs())
        both = (sums[shift].astype(jnp.float32) + arrived.astype(jnp.float32)).astype(jnp.bfloat16)
        if shift:
            both = lax.ppermute(both, "seg", shift_pairs("yx", shift))
        parts.append(both)
    parts, others = lax.optimization_barrier((parts, others))
    rows = STEM_ROWS
    terms = []
    for shift in range(SIDE):
        cut = slice(shift * rows, (shift + 1) * rows)
        total = sum(part[cut].astype(jnp.float32) for part in parts).astype(jnp.bfloat16)
        if shift:
            total = lax.ppermute(total, "seg", shift_pairs("xy", shift))
        terms.append(total)
    return terms, others


def stem_place(node, chip_x, chip_y, sign):
    device = node // NODES_DEV
    x = device // (2 * SIDE)
    y = device // 2 % SIDE
    core = device % 2
    rel_x = (sign * (x - chip_x) + SIDE) % SIDE
    rel_y = (sign * (y - chip_y) + SIDE) % SIDE
    spot = jnp.where(core == 0, rel_y * SIDE + rel_x, rel_x * SIDE + rel_y)
    return core, spot * STEMS + node % NODES_DEV


def part_of(slot):
    return jnp.where(slot == 3, 0, jnp.where(slot == 2, 3, 2 - slot))


def grads_kernel(
    info,
    q_hbm,
    g_hbm,
    k_hbm,
    v_hbm,
    m0_ref,
    m1_ref,
    m2_ref,
    m3_ref,
    o0_ref,
    o1_ref,
    o2_ref,
    o3_ref,
    dq0_ref,
    dq1_ref,
    dq2_ref,
    dq3_ref,
    own_ref,
    sm0_ref,
    sm1_ref,
    sm2_ref,
    sm3_ref,
    so0_ref,
    so1_ref,
    so2_ref,
    so3_ref,
    acc,
    dq_buf,
    stems,
    q_buf,
    g_buf,
    kv_buf,
    sems,
    kv_sems,
):
    seg = info[NODES]
    kv = info[NODES + 1]
    chip_x = seg // (2 * SIDE)
    chip_y = seg // 2 % SIDE
    my_core = seg % 2

    def local_of(step):
        return (kv + part_of(step // 2)) % N_KV * 2 + step % 2

    def local_of(step):
        return (kv + part_of(step // 2)) % N_KV * 2 + step % 2

    def node_copies(step):
        rows = pl.ds(pl.multiple_of(local_of(step) * NODE_LEN, NODE_LEN), NODE_LEN)
        return [
            pltpu.make_async_copy(source.at[rows, :], target.at[step], sems.at[i, step])
            for i, (source, target) in enumerate(((q_hbm, q_buf), (g_hbm, g_buf)))
        ]

    kv_copies = [
        pltpu.make_async_copy(source, kv_buf.at[i], kv_sems.at[i])
        for i, source in enumerate((k_hbm, v_hbm))
    ]
    for copy in node_copies(0) + kv_copies:
        copy.start()
    pieces = (m0_ref, m1_ref, m2_ref, m3_ref, o0_ref, o1_ref, o2_ref, o3_ref)
    for i, piece in enumerate(pieces):
        stems[i * PIECE : (i + 1) * PIECE] = piece[...]

    acc[...] = jnp.zeros(acc.shape, acc.dtype)
    for copy in kv_copies:
        copy.wait()
    for step in range(1, NODES_DEV):
        for copy in node_copies(step):
            copy.start()

    def one_node(step, carry):
        slot = step // 2
        local = local_of(step)
        node_rows = pl.ds(pl.multiple_of(local * NODE_LEN, NODE_LEN), NODE_LEN)
        chain = []
        current = seg * NODES_DEV + local
        count = jnp.int32(0)
        for _ in range(DEPTH - 1):
            current = jnp.where(current >= 0, info[jnp.maximum(current, 0)], -1)
            chain.append(jnp.maximum(current, 0))
            count = count + (current >= 0).astype(jnp.int32)

        for copy in node_copies(step):
            copy.wait()

        def stem_block(ancestor):
            core, spot = stem_place(ancestor, chip_x, chip_y, -1)
            return stems[jnp.where(core == my_core, 0, HALF_STEMS) + spot]

        def run(live):
            keys = [kv_buf[0, node_rows, :]]
            vals = [kv_buf[1, node_rows, :]]
            for j in range(live):
                fetched = stem_block(chain[j])
                keys.append(fetched[:, :D_HEAD])
                vals.append(fetched[:, D_HEAD:])
            keys = jnp.concatenate(keys, axis=0)
            vals = jnp.concatenate(vals, axis=0)
            columns = [slice(h * D_HEAD, (h + 1) * D_HEAD) for h in range(GROUP)]
            q_all = jnp.concatenate([q_buf[step, :, c] for c in columns], axis=0)
            g_all = jnp.concatenate([g_buf[step, :, c] for c in columns], axis=0)
            nt = (((1,), (1,)), ((), ()))
            scores = lax.dot_general(keys, q_all, nt, preferred_element_type=jnp.float32)
            key_pos = lax.broadcasted_iota(jnp.int32, (NODE_LEN, WIDTH), 0)
            query_pos = lax.broadcasted_iota(jnp.int32, (NODE_LEN, WIDTH), 1) & (NODE_LEN - 1)
            own_scores = jnp.where(key_pos <= query_pos, scores[:NODE_LEN], -jnp.inf)
            if live:
                scores = jnp.concatenate([own_scores, scores[NODE_LEN:]], axis=0)
            else:
                scores = own_scores
            top = jnp.max(scores, axis=0, keepdims=True)
            weights = jnp.exp2((scores - top) * EXP2_SCALE)
            prob = weights * (1.0 / jnp.sum(weights, axis=0, keepdims=True))
            prob_half = prob.astype(jnp.bfloat16)
            prob_grads = lax.dot_general(vals, g_all, nt, preferred_element_type=jnp.float32)
            delta = jnp.sum(prob * prob_grads, axis=0, keepdims=True)
            score_half = (prob * (prob_grads - delta)).astype(jnp.bfloat16)
            dq_t = jnp.dot(keys.T, score_half, preferred_element_type=jnp.float32) * SCALE
            for c in columns:
                dq_buf[:, c] = dq_t[:, c].T.astype(jnp.bfloat16)
            dk = jnp.dot(score_half, q_all, preferred_element_type=jnp.float32)
            dv = jnp.dot(prob_half, g_all, preferred_element_type=jnp.float32)
            own_ref[local] = jnp.concatenate([dk[:NODE_LEN], dv[:NODE_LEN]], axis=1)
            for j in range(live):
                core, spot = stem_place(chain[j], chip_x, chip_y, 1)
                place = jnp.where(core == my_core, 0, HALF_STEMS) + spot
                rows = slice((j + 1) * NODE_LEN, (j + 2) * NODE_LEN)
                term = jnp.concatenate([dk[rows], dv[rows]], axis=1)
                acc[place] = (acc[place].astype(jnp.float32) + term).astype(jnp.bfloat16)

        for live in range(DEPTH):
            pl.when(count == live)(functools.partial(run, live))

        block_rows = pl.ds(pl.multiple_of(step % 2 * NODE_LEN, NODE_LEN), NODE_LEN)
        for want, ref in ((0, dq2_ref), (1, dq1_ref), (2, dq3_ref), (3, dq0_ref)):

            @pl.when(slot == want)
            def _(ref=ref):
                ref[block_rows, :] = dq_buf[...]

        return carry

    lax.fori_loop(0, NODES_DEV, one_node, 0)

    sums = (sm0_ref, sm1_ref, sm2_ref, sm3_ref, so0_ref, so1_ref, so2_ref, so3_ref)
    for i, ref in enumerate(sums):
        ref[...] = acc[i * PIECE : (i + 1) * PIECE]


def node_grads(info, queries, out_grad, keys, values, pieces):
    stem_shape = (PIECE, NODE_LEN, 2 * D_HEAD)
    block = jax.ShapeDtypeStruct((BLOCK_ROWS, WIDTH), jnp.bfloat16)
    stay = [
        pltpu.with_memory_space_constraint(array, pltpu.HBM)
        for array in (queries, out_grad, keys, values)
    ]
    smem = pl.BlockSpec(memory_space=pltpu.SMEM)
    vmem = pl.BlockSpec(memory_space=pltpu.VMEM)
    return pl.pallas_call(
        grads_kernel,
        in_specs=[smem] + [pl.BlockSpec(memory_space=pltpu.HBM)] * 4 + [vmem] * (2 * SIDE),
        out_specs=[vmem] * (5 + 2 * SIDE),
        out_shape=[
            block,
            block,
            block,
            block,
            jax.ShapeDtypeStruct((NODES_DEV, NODE_LEN, 2 * D_HEAD), jnp.float32),
        ]
        + [jax.ShapeDtypeStruct(stem_shape, jnp.bfloat16)] * (2 * SIDE),
        scratch_shapes=[
            pltpu.VMEM((2 * HALF_STEMS, NODE_LEN, 2 * D_HEAD), jnp.bfloat16),
            pltpu.VMEM((NODE_LEN, WIDTH), jnp.bfloat16),
            pltpu.VMEM((2 * HALF_STEMS, NODE_LEN, 2 * D_HEAD), jnp.bfloat16),
            pltpu.VMEM((NODES_DEV, NODE_LEN, WIDTH), jnp.bfloat16),
            pltpu.VMEM((NODES_DEV, NODE_LEN, WIDTH), jnp.bfloat16),
            pltpu.VMEM((2, ROWS, D_HEAD), jnp.bfloat16),
            pltpu.SemaphoreType.DMA((2, NODES_DEV)),
            pltpu.SemaphoreType.DMA((2,)),
        ],
        compiler_params=pltpu.CompilerParams(vmem_limit_bytes=40 * 1024 * 1024),
        name="node_grads",
    )(info, *stay, *pieces)


def block_copy(where, shift, ref, out, sem):
    column = pl.multiple_of((where[1] - shift + N_KV) % N_KV * WIDTH, D_HEAD)
    return pltpu.make_async_copy(ref, out.at[:, pl.ds(column, WIDTH)], sem)


def place_kernel(where, a0, a2, own_ref, dq_ref, dk_ref, dv_ref, dk_buf, dv_buf, sems):
    copies = [
        block_copy(where, shift, ref, dq_ref, sems.at[i])
        for i, (shift, ref) in enumerate(((0, a0), (2, a2)))
    ]
    for copy in copies:
        copy.start()
    own = own_ref[STEM_ROWS:]
    dk_buf[...] = (own[:, :D_HEAD] * SCALE).astype(jnp.bfloat16)
    dv_buf[...] = own[:, D_HEAD:].astype(jnp.bfloat16)
    for i, (buf, ref) in enumerate(((dk_buf, dk_ref), (dv_buf, dv_ref))):
        copies.append(pltpu.make_async_copy(buf, ref.at[STEM_ROWS:], sems.at[2 + i]))
        copies[-1].start()
    for copy in copies:
        copy.wait()


def place_first(where, own_block, far_block, own):
    vmem = pl.BlockSpec(memory_space=pltpu.VMEM)
    hbm = pl.BlockSpec(memory_space=pltpu.HBM)
    shape = jax.ShapeDtypeStruct((ROWS, D_HEAD), jnp.bfloat16)
    buf = pltpu.VMEM((ROWS - STEM_ROWS, D_HEAD), jnp.bfloat16)
    return pl.pallas_call(
        place_kernel,
        in_specs=[pl.BlockSpec(memory_space=pltpu.SMEM)] + [vmem] * 3,
        out_specs=[hbm] * 3,
        out_shape=[jax.ShapeDtypeStruct((BLOCK_ROWS, N_KV * WIDTH), jnp.bfloat16), shape, shape],
        scratch_shapes=[buf, buf, pltpu.SemaphoreType.DMA((4,))],
        name="place_first",
    )(where, own_block, far_block, own)


def total_kernel(
    where, a1, a3, own_ref, t0, t1, t2, t3, dq_in, dk_in, dv_in, dq_ref, dk_ref, dv_ref, dk_buf, dv_buf, sems
):
    del dq_in, dk_in, dv_in
    copies = [
        block_copy(where, shift, ref, dq_ref, sems.at[i])
        for i, (shift, ref) in enumerate(((1, a1), (3, a3)))
    ]
    for copy in copies:
        copy.start()
    total = own_ref[:STEM_ROWS] + sum(ref[...].astype(jnp.float32) for ref in (t0, t1, t2, t3))
    dk_buf[...] = (total[:, :D_HEAD] * SCALE).astype(jnp.bfloat16)
    dv_buf[...] = total[:, D_HEAD:].astype(jnp.bfloat16)
    for i, (buf, ref) in enumerate(((dk_buf, dk_ref), (dv_buf, dv_ref))):
        copies.append(pltpu.make_async_copy(buf, ref.at[:STEM_ROWS], sems.at[2 + i]))
        copies[-1].start()
    for copy in copies:
        copy.wait()


def place_last(where, near_blocks, own, terms, placed):
    vmem = pl.BlockSpec(memory_space=pltpu.VMEM)
    hbm = pl.BlockSpec(memory_space=pltpu.HBM)
    buf = pltpu.VMEM((STEM_ROWS, D_HEAD), jnp.bfloat16)
    return pl.pallas_call(
        total_kernel,
        in_specs=[pl.BlockSpec(memory_space=pltpu.SMEM)] + [vmem] * 7 + [hbm] * 3,
        out_specs=[hbm] * 3,
        out_shape=[jax.ShapeDtypeStruct(array.shape, array.dtype) for array in placed],
        scratch_shapes=[buf, buf, pltpu.SemaphoreType.DMA((4,))],
        input_output_aliases={8: 0, 9: 1, 10: 2},
        name="place_last",
    )(where, *near_blocks, own, *terms, *placed)


def per_device(queries, keys, values, out_grad, parents):
    where = jnp.stack([lax.axis_index("seg"), lax.axis_index("kv")]).astype(jnp.int32)
    info = jnp.concatenate([parents, where])
    stem_block = jnp.concatenate([keys[:STEM_ROWS], values[:STEM_ROWS]], axis=1)
    pieces = gather_stems(stem_block)
    dq0, dq1, dq2, dq3, own, *sums = node_grads(
        info, queries, out_grad, keys, values, pieces
    )
    own = own.reshape(ROWS, 2 * D_HEAD)
    near, far, back = (
        lax.ppermute(block, "kv", kv_pairs(shift))
        for shift, block in ((1, dq1), (2, dq2), (3, dq3))
    )
    terms, (far,) = reduce_stems(sums, [far])
    placed = place_first(where, dq0, far, own)
    return tuple(place_last(where, (near, back), own, terms, placed))


def solution(mesh):
    placed = (P("seg", "kv"), P("seg", "kv"), P("seg", "kv"), P("seg", "kv"), P())
    return jax.shard_map(
        per_device,
        mesh=mesh,
        in_specs=placed,
        out_specs=(P(("seg", "kv"), None), P("seg", "kv"), P("seg", "kv")),
        check_vma=False,
    )
```

```python
import functools

import jax
import jax.numpy as jnp
from jax import lax
from jax.experimental import pallas as pl
from jax.experimental.pallas import tpu as pltpu
from jax.sharding import PartitionSpec as P

D_HEAD = 128
GROUP = 7
NODE_LEN = 128
NODES_DEV = 8
STEMS = 2
DEPTH = 6
SIDE = 4
N_SEG = 32
N_KV = 4
ROWS = NODES_DEV * NODE_LEN
STEM_ROWS = STEMS * NODE_LEN
NODES = 256
HALF_STEMS = SIDE * SIDE * STEMS
PIECE = SIDE * STEMS
BLOCK_ROWS = ROWS // N_KV
WIDTH = GROUP * D_HEAD
SCALE = D_HEAD ** (-0.5)
EXP2_SCALE = SCALE * 1.4426950408889634
SHIFTS = (1, 3, 2)


def seg_index(x, y, core):
    return ((x % SIDE) * SIDE + y % SIDE) * 2 + core % 2


def shift_pairs(axis_of_core, shift):
    pairs = []
    for x in range(SIDE):
        for y in range(SIDE):
            for core in range(2):
                dx, dy = (shift, 0) if axis_of_core[core] == "x" else (0, shift)
                pairs.append((seg_index(x, y, core), seg_index(x + dx, y + dy, core)))
    return pairs


def core_pairs():
    return [(i, i ^ 1) for i in range(N_SEG)]


def kv_pairs(shift):
    return [(i, (i + shift) % N_KV) for i in range(N_KV)]


def spread(block, axis_of_core):
    parts = [block] + [
        lax.ppermute(block, "seg", shift_pairs(axis_of_core, shift)) for shift in range(1, SIDE)
    ]
    return jnp.concatenate(parts, axis=0)


def gather_stems(block):
    line = spread(block, "xy")
    parts = [line] + [
        lax.ppermute(line, "seg", shift_pairs("yx", shift)) for shift in range(1, SIDE)
    ]
    swapped = [lax.ppermute(part, "seg", core_pairs()) for part in parts]
    shape = (PIECE, NODE_LEN, 2 * D_HEAD)
    return [part.reshape(shape) for part in parts + swapped]


def reduce_stems(sums, others):
    flat = (PIECE * NODE_LEN, 2 * D_HEAD)
    sums = [term.reshape(flat) for term in sums]
    parts = []
    for shift in (2, 1, 3, 0):
        arrived = lax.ppermute(sums[SIDE + shift], "seg", core_pairs())
        both = (sums[shift].astype(jnp.float32) + arrived.astype(jnp.float32)).astype(jnp.bfloat16)
        if shift:
            both = lax.ppermute(both, "seg", shift_pairs("yx", shift))
        parts.append(both)
    parts, others = lax.optimization_barrier((parts, others))
    rows = STEM_ROWS
    terms = []
    for shift in range(SIDE):
        cut = slice(shift * rows, (shift + 1) * rows)
        total = sum(part[cut].astype(jnp.float32) for part in parts).astype(jnp.bfloat16)
        if shift:
            total = lax.ppermute(total, "seg", shift_pairs("xy", shift))
        terms.append(total)
    return terms, others


def stem_place(node, chip_x, chip_y, sign):
    device = node // NODES_DEV
    x = device // (2 * SIDE)
    y = device // 2 % SIDE
    core = device % 2
    rel_x = (sign * (x - chip_x) + SIDE) % SIDE
    rel_y = (sign * (y - chip_y) + SIDE) % SIDE
    spot = jnp.where(core == 0, rel_y * SIDE + rel_x, rel_x * SIDE + rel_y)
    return core, spot * STEMS + node % NODES_DEV


def grads_kernel(
    info,
    q_hbm,
    g_hbm,
    k_hbm,
    v_hbm,
    m0_ref,
    m1_ref,
    m2_ref,
    m3_ref,
    o0_ref,
    o1_ref,
    o2_ref,
    o3_ref,
    dq0_ref,
    dq1_ref,
    dq2_ref,
    dq3_ref,
    own_ref,
    sm0_ref,
    sm1_ref,
    sm2_ref,
    sm3_ref,
    so0_ref,
    so1_ref,
    so2_ref,
    so3_ref,
    acc,
    dq_buf,
    stems,
    q_buf,
    g_buf,
    kv_buf,
    sems,
    kv_sems,
    counts,
    order,
):
    seg = info[NODES]
    kv = info[NODES + 1]
    chip_x = seg // (2 * SIDE)
    chip_y = seg // 2 % SIDE
    my_core = seg % 2

    def node_copies(local):
        start = local * NODE_LEN
        if not isinstance(local, int):
            start = pl.multiple_of(start, NODE_LEN)
        rows = pl.ds(start, NODE_LEN)
        return [
            pltpu.make_async_copy(source.at[rows, :], target.at[local], sems.at[i, local])
            for i, (source, target) in enumerate(((q_hbm, q_buf), (g_hbm, g_buf)))
        ]

    kv_copies = [
        pltpu.make_async_copy(source, kv_buf.at[i], kv_sems.at[i])
        for i, source in enumerate((k_hbm, v_hbm))
    ]
    for copy in kv_copies:
        copy.start()
    def ancestors(local):
        chain = []
        current = seg * NODES_DEV + local
        count = jnp.int32(0)
        for _ in range(DEPTH - 1):
            current = jnp.where(current >= 0, info[jnp.maximum(current, 0)], -1)
            chain.append(jnp.maximum(current, 0))
            count = count + (current >= 0).astype(jnp.int32)
        return chain, count

    for local in range(NODES_DEV):
        counts[local] = ancestors(local)[1]
    for local in range(NODES_DEV):
        before = jnp.int32(0)
        for other in range(NODES_DEV):
            if other < local:
                before = before + (counts[other] >= counts[local]).astype(jnp.int32)
            elif other > local:
                before = before + (counts[other] > counts[local]).astype(jnp.int32)
        order[before] = local

    for spot in range(2):
        for copy in node_copies(order[spot]):
            copy.start()
    pieces = (m0_ref, m1_ref, m2_ref, m3_ref, o0_ref, o1_ref, o2_ref, o3_ref)
    for i, piece in enumerate(pieces):
        stems[i * PIECE : (i + 1) * PIECE] = piece[...]

    acc[...] = jnp.zeros(acc.shape, acc.dtype)
    for copy in kv_copies:
        copy.wait()
    for spot in range(2, NODES_DEV):
        for copy in node_copies(order[spot]):
            copy.start()

    def one_pair(pair, carry):
        locals_ = [order[2 * pair + i] for i in range(2)]
        found = [ancestors(local) for local in locals_]
        chains = [chain for chain, _ in found]
        live_counts = [count for _, count in found]
        node_rows = [pl.ds(pl.multiple_of(local * NODE_LEN, NODE_LEN), NODE_LEN) for local in locals_]
        for local in locals_:
            for copy in node_copies(local):
                copy.wait()

        def stem_block(ancestor):
            core, spot = stem_place(ancestor, chip_x, chip_y, -1)
            return stems[jnp.where(core == my_core, 0, HALF_STEMS) + spot]

        def run(live):
            columns = [slice(h * D_HEAD, (h + 1) * D_HEAD) for h in range(GROUP)]
            nt = (((1,), (1,)), ((), ()))
            two = range(2)
            keys, vals, q_all, g_all = [], [], [], []
            for i in two:
                fetched = [stem_block(chains[i][j]) for j in range(live)]
                own_k = [kv_buf[0, node_rows[i], :]]
                own_v = [kv_buf[1, node_rows[i], :]]
                keys.append(jnp.concatenate(own_k + [f[:, :D_HEAD] for f in fetched], axis=0))
                vals.append(jnp.concatenate(own_v + [f[:, D_HEAD:] for f in fetched], axis=0))
                q_all.append(jnp.concatenate([q_buf[locals_[i], :, c] for c in columns], axis=0))
                g_all.append(jnp.concatenate([g_buf[locals_[i], :, c] for c in columns], axis=0))

            def masked_scores(i):
                scores = lax.dot_general(keys[i], q_all[i], nt, preferred_element_type=jnp.float32)
                key_pos = lax.broadcasted_iota(jnp.int32, (NODE_LEN, NODE_LEN), 0)
                query_pos = lax.broadcasted_iota(jnp.int32, (NODE_LEN, NODE_LEN), 1)
                causal = key_pos <= query_pos
                own = [jnp.where(causal, scores[:NODE_LEN, c], -jnp.inf) for c in columns]
                parts = [jnp.concatenate(own, axis=1)]
                for j in range(live):
                    part = scores[(j + 1) * NODE_LEN : (j + 2) * NODE_LEN]
                    if i:
                        part = jnp.where(j < live_counts[i], part, -jnp.inf)
                    parts.append(part)
                return jnp.concatenate(parts, axis=0)

            def probs(scores):
                top = jnp.max(scores, axis=0, keepdims=True)
                weights = jnp.exp2((scores - top) * EXP2_SCALE)
                return weights * (1.0 / jnp.sum(weights, axis=0, keepdims=True))

            def prob_slopes(i):
                return lax.dot_general(vals[i], g_all[i], nt, preferred_element_type=jnp.float32)

            def score_slopes(prob, prob_grads):
                delta = jnp.sum(prob * prob_grads, axis=0, keepdims=True)
                return (prob * (prob_grads - delta)).astype(jnp.bfloat16)

            def finish(i, prob_half, score_half):
                dq_t = jnp.dot(keys[i].T, score_half, preferred_element_type=jnp.float32) * SCALE
                for c in columns:
                    dq_buf[i, :, c] = dq_t[:, c].T.astype(jnp.bfloat16)
                dk = jnp.dot(score_half, q_all[i], preferred_element_type=jnp.float32)
                dv = jnp.dot(prob_half, g_all[i], preferred_element_type=jnp.float32)
                own_ref[locals_[i]] = jnp.concatenate([dk[:NODE_LEN], dv[:NODE_LEN]], axis=1)
                return dk, dv

            score = [masked_scores(i) for i in two]
            prob = [probs(score[i]) for i in two]
            slopes = [prob_slopes(i) for i in two]
            halves = [(prob[i].astype(jnp.bfloat16), score_slopes(prob[i], slopes[i])) for i in two]
            grads = [finish(i, *halves[i]) for i in two]

            for i in two:
                dk, dv = grads[i]
                for j in range(live):
                    core, spot = stem_place(chains[i][j], chip_x, chip_y, 1)
                    place = jnp.where(core == my_core, 0, HALF_STEMS) + spot
                    rows = slice((j + 1) * NODE_LEN, (j + 2) * NODE_LEN)
                    term = jnp.concatenate([dk[rows], dv[rows]], axis=1)
                    acc[place] = (acc[place].astype(jnp.float32) + term).astype(jnp.bfloat16)

        for live in range(DEPTH):
            pl.when(live_counts[0] == live)(functools.partial(run, live))

        for i in range(2):
            part = (locals_[i] // 2 - kv + N_KV) % N_KV
            block_rows = pl.ds(pl.multiple_of(locals_[i] % 2 * NODE_LEN, NODE_LEN), NODE_LEN)
            for want, ref in enumerate((dq0_ref, dq1_ref, dq2_ref, dq3_ref)):

                @pl.when(part == want)
                def _(ref=ref, i=i, block_rows=block_rows):
                    ref[block_rows, :] = dq_buf[i]

        return carry

    lax.fori_loop(0, NODES_DEV // 2, one_pair, 0)

    sums = (sm0_ref, sm1_ref, sm2_ref, sm3_ref, so0_ref, so1_ref, so2_ref, so3_ref)
    for i, ref in enumerate(sums):
        ref[...] = acc[i * PIECE : (i + 1) * PIECE]


def node_grads(info, queries, out_grad, keys, values, pieces):
    stem_shape = (PIECE, NODE_LEN, 2 * D_HEAD)
    block = jax.ShapeDtypeStruct((BLOCK_ROWS, WIDTH), jnp.bfloat16)
    stay = [
        pltpu.with_memory_space_constraint(array, pltpu.HBM)
        for array in (queries, out_grad, keys, values)
    ]
    smem = pl.BlockSpec(memory_space=pltpu.SMEM)
    vmem = pl.BlockSpec(memory_space=pltpu.VMEM)
    return pl.pallas_call(
        grads_kernel,
        in_specs=[smem] + [pl.BlockSpec(memory_space=pltpu.HBM)] * 4 + [vmem] * (2 * SIDE),
        out_specs=[vmem] * (5 + 2 * SIDE),
        out_shape=[
            block,
            block,
            block,
            block,
            jax.ShapeDtypeStruct((NODES_DEV, NODE_LEN, 2 * D_HEAD), jnp.float32),
        ]
        + [jax.ShapeDtypeStruct(stem_shape, jnp.bfloat16)] * (2 * SIDE),
        scratch_shapes=[
            pltpu.VMEM((2 * HALF_STEMS, NODE_LEN, 2 * D_HEAD), jnp.bfloat16),
            pltpu.VMEM((2, NODE_LEN, WIDTH), jnp.bfloat16),
            pltpu.VMEM((2 * HALF_STEMS, NODE_LEN, 2 * D_HEAD), jnp.bfloat16),
            pltpu.VMEM((NODES_DEV, NODE_LEN, WIDTH), jnp.bfloat16),
            pltpu.VMEM((NODES_DEV, NODE_LEN, WIDTH), jnp.bfloat16),
            pltpu.VMEM((2, ROWS, D_HEAD), jnp.bfloat16),
            pltpu.SemaphoreType.DMA((2, NODES_DEV)),
            pltpu.SemaphoreType.DMA((2,)),
            pltpu.SMEM((NODES_DEV,), jnp.int32),
            pltpu.SMEM((NODES_DEV,), jnp.int32),
        ],
        compiler_params=pltpu.CompilerParams(vmem_limit_bytes=40 * 1024 * 1024),
        name="node_grads",
    )(info, *stay, *pieces)


def block_copy(where, shift, ref, out, sem):
    column = pl.multiple_of((where[1] - shift + N_KV) % N_KV * WIDTH, D_HEAD)
    return pltpu.make_async_copy(ref, out.at[:, pl.ds(column, WIDTH)], sem)


def place_kernel(where, a0, a2, own_ref, dq_ref, dk_ref, dv_ref, dk_buf, dv_buf, sems):
    copies = [
        block_copy(where, shift, ref, dq_ref, sems.at[i])
        for i, (shift, ref) in enumerate(((0, a0), (2, a2)))
    ]
    for copy in copies:
        copy.start()
    own = own_ref[STEM_ROWS:]
    dk_buf[...] = (own[:, :D_HEAD] * SCALE).astype(jnp.bfloat16)
    dv_buf[...] = own[:, D_HEAD:].astype(jnp.bfloat16)
    for i, (buf, ref) in enumerate(((dk_buf, dk_ref), (dv_buf, dv_ref))):
        copies.append(pltpu.make_async_copy(buf, ref.at[STEM_ROWS:], sems.at[2 + i]))
        copies[-1].start()
    for copy in copies:
        copy.wait()


def place_first(where, own_block, far_block, own):
    vmem = pl.BlockSpec(memory_space=pltpu.VMEM)
    hbm = pl.BlockSpec(memory_space=pltpu.HBM)
    shape = jax.ShapeDtypeStruct((ROWS, D_HEAD), jnp.bfloat16)
    buf = pltpu.VMEM((ROWS - STEM_ROWS, D_HEAD), jnp.bfloat16)
    return pl.pallas_call(
        place_kernel,
        in_specs=[pl.BlockSpec(memory_space=pltpu.SMEM)] + [vmem] * 3,
        out_specs=[hbm] * 3,
        out_shape=[jax.ShapeDtypeStruct((BLOCK_ROWS, N_KV * WIDTH), jnp.bfloat16), shape, shape],
        scratch_shapes=[buf, buf, pltpu.SemaphoreType.DMA((4,))],
        name="place_first",
    )(where, own_block, far_block, own)


def total_kernel(
    where, a1, a3, own_ref, t0, t1, t2, t3, dq_in, dk_in, dv_in, dq_ref, dk_ref, dv_ref, dk_buf, dv_buf, sems
):
    del dq_in, dk_in, dv_in
    copies = [
        block_copy(where, shift, ref, dq_ref, sems.at[i])
        for i, (shift, ref) in enumerate(((1, a1), (3, a3)))
    ]
    for copy in copies:
        copy.start()
    total = own_ref[:STEM_ROWS] + sum(ref[...].astype(jnp.float32) for ref in (t0, t1, t2, t3))
    dk_buf[...] = (total[:, :D_HEAD] * SCALE).astype(jnp.bfloat16)
    dv_buf[...] = total[:, D_HEAD:].astype(jnp.bfloat16)
    for i, (buf, ref) in enumerate(((dk_buf, dk_ref), (dv_buf, dv_ref))):
        copies.append(pltpu.make_async_copy(buf, ref.at[:STEM_ROWS], sems.at[2 + i]))
        copies[-1].start()
    for copy in copies:
        copy.wait()


def place_last(where, near_blocks, own, terms, placed):
    vmem = pl.BlockSpec(memory_space=pltpu.VMEM)
    hbm = pl.BlockSpec(memory_space=pltpu.HBM)
    buf = pltpu.VMEM((STEM_ROWS, D_HEAD), jnp.bfloat16)
    return pl.pallas_call(
        total_kernel,
        in_specs=[pl.BlockSpec(memory_space=pltpu.SMEM)] + [vmem] * 7 + [hbm] * 3,
        out_specs=[hbm] * 3,
        out_shape=[jax.ShapeDtypeStruct(array.shape, array.dtype) for array in placed],
        scratch_shapes=[buf, buf, pltpu.SemaphoreType.DMA((4,))],
        input_output_aliases={8: 0, 9: 1, 10: 2},
        name="place_last",
    )(where, *near_blocks, own, *terms, *placed)


def per_device(queries, keys, values, out_grad, parents):
    where = jnp.stack([lax.axis_index("seg"), lax.axis_index("kv")]).astype(jnp.int32)
    info = jnp.concatenate([parents, where])
    stem_block = jnp.concatenate([keys[:STEM_ROWS], values[:STEM_ROWS]], axis=1)
    pieces = gather_stems(stem_block)
    dq0, dq1, dq2, dq3, own, *sums = node_grads(
        info, queries, out_grad, keys, values, pieces
    )
    own = own.reshape(ROWS, 2 * D_HEAD)
    near, far, back = (
        lax.ppermute(block, "kv", kv_pairs(shift))
        for shift, block in ((1, dq1), (2, dq2), (3, dq3))
    )
    terms, (far,) = reduce_stems(sums, [far])
    placed = place_first(where, dq0, far, own)
    return tuple(place_last(where, (near, back), own, terms, placed))


def solution(mesh):
    placed = (P("seg", "kv"), P("seg", "kv"), P("seg", "kv"), P("seg", "kv"), P())
    return jax.shard_map(
        per_device,
        mesh=mesh,
        in_specs=placed,
        out_specs=(P(("seg", "kv"), None), P("seg", "kv"), P("seg", "kv")),
        check_vma=False,
    )
```

```python
import functools

import jax
import jax.numpy as jnp
from jax import lax
from jax.experimental import pallas as pl
from jax.experimental.pallas import tpu as pltpu
from jax.sharding import PartitionSpec as P

D_HEAD = 128
GROUP = 7
NODE_LEN = 128
NODES_DEV = 8
STEMS = 2
DEPTH = 6
SIDE = 4
N_SEG = 32
N_KV = 4
ROWS = NODES_DEV * NODE_LEN
STEM_ROWS = STEMS * NODE_LEN
NODES = 256
HALF_STEMS = SIDE * SIDE * STEMS
PIECE = SIDE * STEMS
BLOCK_ROWS = ROWS // N_KV
WIDTH = GROUP * D_HEAD
SCALE = D_HEAD ** (-0.5)
EXP2_SCALE = SCALE * 1.4426950408889634
SEND_ORDER = (1, 3, 2)


def seg_index(x, y, core):
    return ((x % SIDE) * SIDE + y % SIDE) * 2 + core % 2


def shift_pairs(axis_of_core, shift):
    pairs = []
    for x in range(SIDE):
        for y in range(SIDE):
            for core in range(2):
                dx, dy = (shift, 0) if axis_of_core[core] == "x" else (0, shift)
                pairs.append((seg_index(x, y, core), seg_index(x + dx, y + dy, core)))
    return pairs


def core_pairs():
    return [(i, i ^ 1) for i in range(N_SEG)]


def kv_pairs(shift):
    return [(i, (i + shift) % N_KV) for i in range(N_KV)]


def from_line(block, axis_of_core):
    return [block] + [
        lax.ppermute(block, "seg", shift_pairs(axis_of_core, shift)) for shift in SEND_ORDER
    ]


def spread(block, axis_of_core):
    return jnp.concatenate(from_line(block, axis_of_core), axis=0)


def gather_stems(block):
    line = spread(block, "xy")
    parts = from_line(line, "yx")
    swapped = [lax.ppermute(part, "seg", core_pairs()) for part in parts]
    shape = (PIECE, NODE_LEN, 2 * D_HEAD)
    return [part.reshape(shape) for part in parts + swapped]


def reduce_stems(sums, others):
    flat = (PIECE * NODE_LEN, 2 * D_HEAD)
    sums = [term.reshape(flat) for term in sums]
    parts = []
    for shift in (2, 1, 3, 0):
        arrived = lax.ppermute(sums[SIDE + shift], "seg", core_pairs())
        both = (sums[shift].astype(jnp.float32) + arrived.astype(jnp.float32)).astype(jnp.bfloat16)
        if shift:
            both = lax.ppermute(both, "seg", shift_pairs("yx", shift))
        parts.append(both)
    parts, others = lax.optimization_barrier((parts, others))
    rows = STEM_ROWS
    terms = []
    for shift in (0,) + SEND_ORDER:
        cut = slice(shift * rows, (shift + 1) * rows)
        total = sum(part[cut].astype(jnp.float32) for part in parts).astype(jnp.bfloat16)
        if shift:
            total = lax.ppermute(total, "seg", shift_pairs("xy", shift))
        terms.append(total)
    return terms, others


def stem_place(node, chip_x, chip_y, sign):
    device = node // NODES_DEV
    x = device // (2 * SIDE)
    y = device // 2 % SIDE
    core = device % 2
    rel_x = (sign * (x - chip_x) + SIDE) % SIDE
    rel_y = (sign * (y - chip_y) + SIDE) % SIDE
    if sign < 0:
        rel_x = rel_x ^ (rel_x >> 1)
        rel_y = rel_y ^ (rel_y >> 1)
    spot = jnp.where(core == 0, rel_y * SIDE + rel_x, rel_x * SIDE + rel_y)
    return core, spot * STEMS + node % NODES_DEV


def grads_kernel(
    info,
    q_hbm,
    g_hbm,
    k_hbm,
    v_hbm,
    m0_ref,
    m1_ref,
    m2_ref,
    m3_ref,
    o0_ref,
    o1_ref,
    o2_ref,
    o3_ref,
    dq0_ref,
    dq1_ref,
    dq2_ref,
    dq3_ref,
    own_ref,
    sm0_ref,
    sm1_ref,
    sm2_ref,
    sm3_ref,
    so0_ref,
    so1_ref,
    so2_ref,
    so3_ref,
    acc,
    dq_buf,
    stems,
    q_buf,
    g_buf,
    kv_buf,
    sems,
    kv_sems,
    counts,
    order,
):
    seg = info[NODES]
    kv = info[NODES + 1]
    chip_x = seg // (2 * SIDE)
    chip_y = seg // 2 % SIDE
    my_core = seg % 2

    def node_copies(local):
        start = local * NODE_LEN
        if not isinstance(local, int):
            start = pl.multiple_of(start, NODE_LEN)
        rows = pl.ds(start, NODE_LEN)
        return [
            pltpu.make_async_copy(source.at[rows, :], target.at[local], sems.at[i, local])
            for i, (source, target) in enumerate(((q_hbm, q_buf), (g_hbm, g_buf)))
        ]

    kv_copies = [
        pltpu.make_async_copy(source, kv_buf.at[i], kv_sems.at[i])
        for i, source in enumerate((k_hbm, v_hbm))
    ]
    for copy in kv_copies:
        copy.start()
    def ancestors(local):
        chain = []
        current = seg * NODES_DEV + local
        count = jnp.int32(0)
        for _ in range(DEPTH - 1):
            current = jnp.where(current >= 0, info[jnp.maximum(current, 0)], -1)
            chain.append(jnp.maximum(current, 0))
            count = count + (current >= 0).astype(jnp.int32)
        return chain, count

    for local in range(NODES_DEV):
        counts[local] = ancestors(local)[1]
    for local in range(NODES_DEV):
        before = jnp.int32(0)
        for other in range(NODES_DEV):
            if other < local:
                before = before + (counts[other] >= counts[local]).astype(jnp.int32)
            elif other > local:
                before = before + (counts[other] > counts[local]).astype(jnp.int32)
        order[before] = local

    for spot in range(2):
        for copy in node_copies(order[spot]):
            copy.start()
    pieces = (m0_ref, m1_ref, m2_ref, m3_ref, o0_ref, o1_ref, o2_ref, o3_ref)
    for i, piece in enumerate(pieces):
        stems[i * PIECE : (i + 1) * PIECE] = piece[...]

    acc[...] = jnp.zeros(acc.shape, acc.dtype)
    for copy in kv_copies:
        copy.wait()
    for spot in range(2, NODES_DEV):
        for copy in node_copies(order[spot]):
            copy.start()

    def one_pair(pair, carry):
        locals_ = [order[2 * pair + i] for i in range(2)]
        found = [ancestors(local) for local in locals_]
        chains = [chain for chain, _ in found]
        live_counts = [count for _, count in found]
        node_rows = [pl.ds(pl.multiple_of(local * NODE_LEN, NODE_LEN), NODE_LEN) for local in locals_]
        for local in locals_:
            for copy in node_copies(local):
                copy.wait()

        def stem_block(ancestor):
            core, spot = stem_place(ancestor, chip_x, chip_y, -1)
            return stems[jnp.where(core == my_core, 0, HALF_STEMS) + spot]

        def run(live):
            columns = [slice(h * D_HEAD, (h + 1) * D_HEAD) for h in range(GROUP)]
            nt = (((1,), (1,)), ((), ()))
            two = range(2)
            keys, vals, q_all, g_all = [], [], [], []
            for i in two:
                fetched = [stem_block(chains[i][j]) for j in range(live)]
                own_k = [kv_buf[0, node_rows[i], :]]
                own_v = [kv_buf[1, node_rows[i], :]]
                keys.append(jnp.concatenate(own_k + [f[:, :D_HEAD] for f in fetched], axis=0))
                vals.append(jnp.concatenate(own_v + [f[:, D_HEAD:] for f in fetched], axis=0))
                q_all.append(jnp.concatenate([q_buf[locals_[i], :, c] for c in columns], axis=0))
                g_all.append(jnp.concatenate([g_buf[locals_[i], :, c] for c in columns], axis=0))

            def masked_scores(i):
                scores = lax.dot_general(keys[i], q_all[i], nt, preferred_element_type=jnp.float32)
                key_pos = lax.broadcasted_iota(jnp.int32, (NODE_LEN, NODE_LEN), 0)
                query_pos = lax.broadcasted_iota(jnp.int32, (NODE_LEN, NODE_LEN), 1)
                causal = key_pos <= query_pos
                own = [jnp.where(causal, scores[:NODE_LEN, c], -jnp.inf) for c in columns]
                parts = [jnp.concatenate(own, axis=1)]
                for j in range(live):
                    part = scores[(j + 1) * NODE_LEN : (j + 2) * NODE_LEN]
                    if i:
                        part = jnp.where(j < live_counts[i], part, -jnp.inf)
                    parts.append(part)
                return jnp.concatenate(parts, axis=0)

            def probs(scores):
                top = jnp.max(scores, axis=0, keepdims=True)
                weights = jnp.exp2((scores - top) * EXP2_SCALE)
                return weights * (1.0 / jnp.sum(weights, axis=0, keepdims=True))

            def prob_slopes(i):
                return lax.dot_general(vals[i], g_all[i], nt, preferred_element_type=jnp.float32)

            def score_slopes(prob, prob_grads):
                delta = jnp.sum(prob * prob_grads, axis=0, keepdims=True)
                return (prob * (prob_grads - delta)).astype(jnp.bfloat16)

            def finish(i, prob_half, score_half):
                dq_t = jnp.dot(keys[i].T, score_half, preferred_element_type=jnp.float32) * SCALE
                for c in columns:
                    dq_buf[i, :, c] = dq_t[:, c].T.astype(jnp.bfloat16)
                dk = jnp.dot(score_half, q_all[i], preferred_element_type=jnp.float32)
                dv = jnp.dot(prob_half, g_all[i], preferred_element_type=jnp.float32)
                own_ref[locals_[i]] = jnp.concatenate([dk[:NODE_LEN], dv[:NODE_LEN]], axis=1)
                return dk, dv

            score = [masked_scores(i) for i in two]
            prob = [probs(score[i]) for i in two]
            slopes = [prob_slopes(i) for i in two]
            halves = [(prob[i].astype(jnp.bfloat16), score_slopes(prob[i], slopes[i])) for i in two]
            grads = [finish(i, *halves[i]) for i in two]

            for i in two:
                dk, dv = grads[i]
                for j in range(live):
                    core, spot = stem_place(chains[i][j], chip_x, chip_y, 1)
                    place = jnp.where(core == my_core, 0, HALF_STEMS) + spot
                    rows = slice((j + 1) * NODE_LEN, (j + 2) * NODE_LEN)
                    term = jnp.concatenate([dk[rows], dv[rows]], axis=1)
                    acc[place] = (acc[place].astype(jnp.float32) + term).astype(jnp.bfloat16)

        for live in range(DEPTH):
            pl.when(live_counts[0] == live)(functools.partial(run, live))

        for i in range(2):
            part = (locals_[i] // 2 - kv + N_KV) % N_KV
            block_rows = pl.ds(pl.multiple_of(locals_[i] % 2 * NODE_LEN, NODE_LEN), NODE_LEN)
            for want, ref in enumerate((dq0_ref, dq1_ref, dq2_ref, dq3_ref)):

                @pl.when(part == want)
                def _(ref=ref, i=i, block_rows=block_rows):
                    ref[block_rows, :] = dq_buf[i]

        return carry

    lax.fori_loop(0, NODES_DEV // 2, one_pair, 0)

    sums = (sm0_ref, sm1_ref, sm2_ref, sm3_ref, so0_ref, so1_ref, so2_ref, so3_ref)
    for i, ref in enumerate(sums):
        ref[...] = acc[i * PIECE : (i + 1) * PIECE]


def node_grads(info, queries, out_grad, keys, values, pieces):
    stem_shape = (PIECE, NODE_LEN, 2 * D_HEAD)
    block = jax.ShapeDtypeStruct((BLOCK_ROWS, WIDTH), jnp.bfloat16)
    stay = [
        pltpu.with_memory_space_constraint(array, pltpu.HBM)
        for array in (queries, out_grad, keys, values)
    ]
    smem = pl.BlockSpec(memory_space=pltpu.SMEM)
    vmem = pl.BlockSpec(memory_space=pltpu.VMEM)
    return pl.pallas_call(
        grads_kernel,
        in_specs=[smem] + [pl.BlockSpec(memory_space=pltpu.HBM)] * 4 + [vmem] * (2 * SIDE),
        out_specs=[vmem] * (5 + 2 * SIDE),
        out_shape=[
            block,
            block,
            block,
            block,
            jax.ShapeDtypeStruct((NODES_DEV, NODE_LEN, 2 * D_HEAD), jnp.float32),
        ]
        + [jax.ShapeDtypeStruct(stem_shape, jnp.bfloat16)] * (2 * SIDE),
        scratch_shapes=[
            pltpu.VMEM((2 * HALF_STEMS, NODE_LEN, 2 * D_HEAD), jnp.bfloat16),
            pltpu.VMEM((2, NODE_LEN, WIDTH), jnp.bfloat16),
            pltpu.VMEM((2 * HALF_STEMS, NODE_LEN, 2 * D_HEAD), jnp.bfloat16),
            pltpu.VMEM((NODES_DEV, NODE_LEN, WIDTH), jnp.bfloat16),
            pltpu.VMEM((NODES_DEV, NODE_LEN, WIDTH), jnp.bfloat16),
            pltpu.VMEM((2, ROWS, D_HEAD), jnp.bfloat16),
            pltpu.SemaphoreType.DMA((2, NODES_DEV)),
            pltpu.SemaphoreType.DMA((2,)),
            pltpu.SMEM((NODES_DEV,), jnp.int32),
            pltpu.SMEM((NODES_DEV,), jnp.int32),
        ],
        compiler_params=pltpu.CompilerParams(vmem_limit_bytes=40 * 1024 * 1024),
        name="node_grads",
    )(info, *stay, *pieces)


def block_copy(where, shift, ref, out, sem):
    column = pl.multiple_of((where[1] - shift + N_KV) % N_KV * WIDTH, D_HEAD)
    return pltpu.make_async_copy(ref, out.at[:, pl.ds(column, WIDTH)], sem)


def place_kernel(where, a0, a2, own_ref, dq_ref, dk_ref, dv_ref, dk_buf, dv_buf, sems):
    copies = [
        block_copy(where, shift, ref, dq_ref, sems.at[i])
        for i, (shift, ref) in enumerate(((0, a0), (2, a2)))
    ]
    for copy in copies:
        copy.start()
    own = own_ref[STEM_ROWS:]
    dk_buf[...] = (own[:, :D_HEAD] * SCALE).astype(jnp.bfloat16)
    dv_buf[...] = own[:, D_HEAD:].astype(jnp.bfloat16)
    for i, (buf, ref) in enumerate(((dk_buf, dk_ref), (dv_buf, dv_ref))):
        copies.append(pltpu.make_async_copy(buf, ref.at[STEM_ROWS:], sems.at[2 + i]))
        copies[-1].start()
    for copy in copies:
        copy.wait()


def place_first(where, own_block, far_block, own):
    vmem = pl.BlockSpec(memory_space=pltpu.VMEM)
    hbm = pl.BlockSpec(memory_space=pltpu.HBM)
    shape = jax.ShapeDtypeStruct((ROWS, D_HEAD), jnp.bfloat16)
    buf = pltpu.VMEM((ROWS - STEM_ROWS, D_HEAD), jnp.bfloat16)
    return pl.pallas_call(
        place_kernel,
        in_specs=[pl.BlockSpec(memory_space=pltpu.SMEM)] + [vmem] * 3,
        out_specs=[hbm] * 3,
        out_shape=[jax.ShapeDtypeStruct((BLOCK_ROWS, N_KV * WIDTH), jnp.bfloat16), shape, shape],
        scratch_shapes=[buf, buf, pltpu.SemaphoreType.DMA((4,))],
        name="place_first",
    )(where, own_block, far_block, own)


def total_kernel(
    where, a1, a3, own_ref, t0, t1, t2, t3, dq_in, dk_in, dv_in, dq_ref, dk_ref, dv_ref, dk_buf, dv_buf, sems
):
    del dq_in, dk_in, dv_in
    copies = [
        block_copy(where, shift, ref, dq_ref, sems.at[i])
        for i, (shift, ref) in enumerate(((1, a1), (3, a3)))
    ]
    for copy in copies:
        copy.start()
    total = own_ref[:STEM_ROWS] + sum(ref[...].astype(jnp.float32) for ref in (t0, t1, t2, t3))
    dk_buf[...] = (total[:, :D_HEAD] * SCALE).astype(jnp.bfloat16)
    dv_buf[...] = total[:, D_HEAD:].astype(jnp.bfloat16)
    for i, (buf, ref) in enumerate(((dk_buf, dk_ref), (dv_buf, dv_ref))):
        copies.append(pltpu.make_async_copy(buf, ref.at[:STEM_ROWS], sems.at[2 + i]))
        copies[-1].start()
    for copy in copies:
        copy.wait()


def place_last(where, near_blocks, own, terms, placed):
    vmem = pl.BlockSpec(memory_space=pltpu.VMEM)
    hbm = pl.BlockSpec(memory_space=pltpu.HBM)
    buf = pltpu.VMEM((STEM_ROWS, D_HEAD), jnp.bfloat16)
    return pl.pallas_call(
        total_kernel,
        in_specs=[pl.BlockSpec(memory_space=pltpu.SMEM)] + [vmem] * 7 + [hbm] * 3,
        out_specs=[hbm] * 3,
        out_shape=[jax.ShapeDtypeStruct(array.shape, array.dtype) for array in placed],
        scratch_shapes=[buf, buf, pltpu.SemaphoreType.DMA((4,))],
        input_output_aliases={8: 0, 9: 1, 10: 2},
        name="place_last",
    )(where, *near_blocks, own, *terms, *placed)


def per_device(queries, keys, values, out_grad, parents):
    where = jnp.stack([lax.axis_index("seg"), lax.axis_index("kv")]).astype(jnp.int32)
    info = jnp.concatenate([parents, where])
    stem_block = jnp.concatenate([keys[:STEM_ROWS], values[:STEM_ROWS]], axis=1)
    pieces = gather_stems(stem_block)
    dq0, dq1, dq2, dq3, own, *sums = node_grads(
        info, queries, out_grad, keys, values, pieces
    )
    own = own.reshape(ROWS, 2 * D_HEAD)
    near, far, back = (
        lax.ppermute(block, "kv", kv_pairs(shift))
        for shift, block in ((1, dq1), (2, dq2), (3, dq3))
    )
    terms, (far,) = reduce_stems(sums, [far])
    placed = place_first(where, dq0, far, own)
    return tuple(place_last(where, (near, back), own, terms, placed))


def solution(mesh):
    placed = (P("seg", "kv"), P("seg", "kv"), P("seg", "kv"), P("seg", "kv"), P())
    return jax.shard_map(
        per_device,
        mesh=mesh,
        in_specs=placed,
        out_specs=(P(("seg", "kv"), None), P("seg", "kv"), P("seg", "kv")),
        check_vma=False,
    )
```
